512 devices in a mesh: cell: 64 (over z, y), mode: 8 (over x, core).
Axes of the slice: x: 4, y: 4, z: 16, core: 2. Of those that a mesh axis runs over, the one named last changes fastest.
Arguments:
- source: bfloat16 [2048, 64, 1024], P('mode', 'cell'), may hold values from -6 to 6
- prior: bfloat16 [2048, 64, 1024], P('mode', 'cell'), may hold values from -6 to 6
- coupling: bfloat16 [16, 4, 128, 128], P('mode'), may hold values from -0.25 to 0.25
- pairs: int32 [16, 4], replicated, may hold values from 0 to 15, all different within a row
- transmission: float32 [3, 2048], P(None, 'mode'), may hold values from 0 to 1, as said below
- direction: int32 [3, 2048], P(None, 'mode'), may hold values from 0 to 1
Outputs:
- distribution: bfloat16 [2048, 64, 1024], P('mode', 'cell')
The draws below stay inside these ranges and needn't reach their ends.
Inputs may be any that keep to these rules, and one draw needn't show every extreme that they name: Each row of pairs names 4 different column blocks, and every column block is named by some row. `transmission`: each entry lies strictly between 0 and 1.
All inputs are finite; a program needn't handle non-finite values.
Results may differ from the reference program's by a relative error of at most 0.0023.
Values may be sent and summed in bfloat16 or wider, within the bound.
A program may use at most 64 MiB of HBM per device.

```python
import jax
import jax.numpy as jnp
from jax import lax

MODES = 2048
BLOCK = 128
PER_ROW = 4
ITERS = 2
NY = 32
NZ = 32
NBLK = 16
NX = 64
PLANE = 1024


def draw_transmission(key, part):
    key = jax.random.fold_in(key, 7)
    lengths = jnp.array([NX, NY, NZ], jnp.float32)[:, None]
    reach = jnp.exp(jax.random.uniform(key, (3, MODES), jnp.float32, jnp.log(0.2), jnp.log(20.0)))
    return jnp.exp(-reach / lengths)


def plant(drawn, key, low, largest):
    shape = drawn.shape
    spot = [jax.random.randint(jax.random.fold_in(key, axis), (), 0, shape[axis]) for axis in range(len(shape))]
    drawn = drawn.at[tuple(spot)].set(low)
    longest = shape.index(max(shape))
    spot[longest] = (spot[longest] + 1) % shape[longest]
    return drawn.at[tuple(spot)].set(largest)


def levels(stream_key, dims, split, low, top_value):
    def one(position, parts):
        draws = jax.random.uniform(jax.random.fold_in(jax.random.fold_in(stream_key, 6), position), (parts,), jnp.float32, low / len(split), top_value / len(split))
        return jnp.repeat(jnp.exp(draws), dims[position] // parts).reshape((-1,) + (1,) * (len(dims) - position - 1))

    loudness = one(*split[0])
    for cut in split[1:]:
        loudness = loudness * one(*cut)
    return loudness


def choose_distinct(rng, rows, number_of, top, lift):
    order = jax.random.permutation(jax.random.fold_in(rng, 1), number_of)
    pull = order
    for power in range(3):
        pull = pull * pull // number_of
    pull = pull * lift // number_of
    lots = jax.random.randint(jax.random.fold_in(rng, 2), (rows, number_of), 0, 4096) + pull
    sure = jax.random.permutation(jax.random.fold_in(rng, 3), rows)[jnp.arange(number_of) % rows]
    lots = jnp.where(jnp.arange(rows)[:, None] == sure[None, :], 1 << 14, lots)
    merit = lots * number_of + jnp.arange(number_of)
    return lax.top_k(merit.astype(jnp.int32), top)[1].astype(jnp.int32)


def centred(own_key, extent, deviation, limit, cuts=(), kind=jnp.bfloat16):
    loudness = levels(own_key, extent, cuts, -0.22, 0.18) if cuts else 1.0
    result = jax.random.normal(own_key, extent, jnp.float32) * deviation * loudness
    return jnp.minimum(jnp.maximum(result, -limit), limit).astype(kind)


def setup_inputs(seed: int = 0) -> dict:
    streams_of = jax.random.split(jax.random.key(seed), 7)
    return {
        "source": centred(streams_of[0], (MODES, NX, PLANE), 1.0, 6.0, ((0, 8), (1, 64))),
        "prior": centred(streams_of[1], (MODES, NX, PLANE), 1.0, 6.0, ((0, 8), (1, 64))),
        "coupling": centred(streams_of[2], (NBLK, PER_ROW, BLOCK, BLOCK), (PER_ROW * BLOCK) ** -0.5, 0.25, ((0, 8),)),
        "pairs": choose_distinct(streams_of[3], NBLK, NBLK, PER_ROW, 4096),
        "transmission": draw_transmission(jax.random.fold_in(streams_of[6], 71), 0),
        "direction": plant(jax.random.randint(streams_of[5], (3, MODES), 0, 2), jax.random.fold_in(streams_of[5], 1), 0, 1).astype(jnp.int32),
    }


def sweep_axis(volume, decay_rate, forward, along):
    reordered = jnp.moveaxis(volume, along, 0)
    shaped = (decay_rate.shape[0], 1, 1)
    factor = decay_rate.reshape(shaped)
    forward_mask = forward.reshape(shaped) == 1
    ordered = jnp.where(forward_mask, reordered, reordered[::-1])
    weight = jnp.sqrt(1.0 - factor * factor)

    def advance(carried, entry_value):
        carried = factor * carried + weight * entry_value
        return (carried, carried)
    _, swept_rows = lax.scan(advance, jnp.zeros_like(ordered[0]), ordered)
    swept_rows = jnp.where(forward_mask, swept_rows, swept_rows[::-1])
    return jnp.moveaxis(swept_rows, 0, along)

def stream_block(packed):
    volume, decay_rate, forward = packed
    volume = sweep_axis(volume, decay_rate[0], forward[0], 1)
    volume = sweep_axis(volume, decay_rate[1], forward[1], 2)
    volume = sweep_axis(volume, decay_rate[2], forward[2], 3)
    return volume

def stream(right_side, transmission, direction):
    blocks = right_side.reshape(NBLK, BLOCK, NX, NY, NZ)
    decays = transmission.reshape(3, NBLK, BLOCK).transpose(1, 0, 2)
    senses = direction.reshape(3, NBLK, BLOCK).transpose(1, 0, 2)
    swept_rows = lax.map(stream_block, (blocks, decays, senses))
    return swept_rows.reshape(MODES, NX, NY * NZ)

def couple(current, coupling, pairs):
    flat_rows = current.reshape(NBLK, BLOCK, NX * NY * NZ)

    def one_row(row_index):
        picked = jnp.take(flat_rows, pairs[row_index], axis=0).reshape(PER_ROW * BLOCK, NX * NY * NZ)
        left_side = coupling[row_index].transpose(1, 0, 2).reshape(BLOCK, PER_ROW * BLOCK)
        return jnp.dot(left_side, picked, preferred_element_type=jnp.float32)
    row_list = lax.map(one_row, jnp.arange(NBLK, dtype=jnp.int32))
    return row_list.reshape(MODES, NX, NY * NZ)

def reference(source, prior, coupling, pairs, transmission, direction):
    current = prior
    emission = source.astype(jnp.float32)
    for iteration in range(ITERS):
        right_side = emission + couple(current, coupling, pairs)
        current = stream(right_side, transmission, direction).astype(jnp.bfloat16)
    return current
```

```python
import functools

import jax
import jax.numpy as jnp
from jax import lax
from jax.experimental import pallas as pl
from jax.experimental.pallas import tpu as pltpu
from jax.sharding import PartitionSpec as P

ITERS = 2
BLOCK = 128
PER_ROW = 4
ZLO = 8
YLO = 4
XLO = 4
TOP = 32767.0
F32 = jnp.float32
BF16 = jnp.bfloat16
I16 = jnp.int16
MESH = pl.DeviceIdType.MESH


def nt(left, right):
    return lax.dot_general(left, right, (((1,), (1,)), ((), ())), preferred_element_type=F32)


def identity(size):
    rows = lax.broadcasted_iota(jnp.int32, (size, size), 0)
    columns = lax.broadcasted_iota(jnp.int32, (size, size), 1)
    return jnp.where(rows == columns, 1.0, 0.0).astype(BF16)


def run(values, factor, forward):
    n = len(values)
    ordered = [jnp.where(forward, values[s], values[n - 1 - s]) for s in range(n)]
    swept = [ordered[0]]
    for s in range(1, n):
        swept.append(factor * swept[-1] + ordered[s])
    return [jnp.where(forward, swept[s], swept[n - 1 - s]) for s in range(n)]


def encode(values, scale):
    return jnp.round(values * scale).astype(jnp.int32).astype(I16)


def decode(codes):
    return codes.astype(jnp.int32).astype(F32)


def kernel(
    dims,
    source,
    prior,
    coupling,
    pairs,
    transmission,
    direction,
    out,
    cur_a,
    cur_b,
    emission,
    turned,
    turned_s,
    blocks,
    coef_own,
    coef,
    work,
    x_send,
    x_recv,
    xs_send,
    xs_recv,
    planes,
    ends,
    e_send,
    e_recv,
    es_send,
    es_recv,
    b_send,
    b_recv,
    bs_send,
    bs_recv,
    c_send,
    f_send,
    f_recv,
    s0_send,
    s0_recv,
    gather_send,
    gather_recv,
    x_sem,
    e_sem,
    b_sem,
    c_sem,
    f_sem,
    scale_sem,
):
    nm, ny_dev, nz_dev, ny, nz = dims
    chips = nm // 2
    chunk = YLO * nz
    tall = ny * ZLO
    per_z = tall // nz_dev
    me_m = lax.axis_index("mode")
    me_c = lax.axis_index("cell")
    me_z, me_y = me_c // ny_dev, me_c % ny_dev
    me_x, me_core = me_m // 2, me_m % 2

    def remote(src, dst, send, recv, to):
        return pltpu.make_async_remote_copy(
            src_ref=src, dst_ref=dst, send_sem=send, recv_sem=recv, device_id=to, device_id_type=MESH
        )

    def await_bytes(ref, sem):
        pltpu.make_async_copy(ref, ref, sem).wait()

    barrier = pltpu.get_barrier_semaphore()
    group = nm * ny_dev

    def greet_group(j, carry):
        m = (me_m + j // ny_dev) % nm
        y = (me_y + j % ny_dev) % ny_dev
        pl.semaphore_signal(barrier, inc=1, device_id=(me_z * ny_dev + y, m), device_id_type=MESH)
        return carry

    lax.fori_loop(1, group, greet_group, 0)

    def greet_ring(j, carry):
        z = (me_z + j) % nz_dev
        pl.semaphore_signal(barrier, inc=1, device_id=(z * ny_dev + me_y, me_m), device_id_type=MESH)
        return carry

    lax.fori_loop(1, nz_dev, greet_ring, 0)

    fwd = {}
    fac = {}
    weight = {}
    for h in range(2):
        lanes = slice(h * BLOCK, (h + 1) * BLOCK)
        for d in range(3):
            fac[d, h] = jnp.broadcast_to(transmission[d : d + 1, lanes], (8, BLOCK))
            fwd[d, h] = jnp.broadcast_to(direction[d : d + 1, lanes], (8, BLOCK)) == 1
        total = jnp.sqrt(1.0 - transmission[0:1, lanes] * transmission[0:1, lanes])
        for d in range(1, 3):
            total = total * jnp.sqrt(1.0 - transmission[d : d + 1, lanes] * transmission[d : d + 1, lanes])
        weight[h] = total
    for h in range(2):
        coef_own[0, h * 4 : h * 4 + 4, :] = fac[2, h][:4]
        coef_own[1, h * 4 : h * 4 + 4, :] = jnp.where(fwd[2, h], 1.0, 0.0)[:4]

    eye = identity(chunk)

    def turn(array, into):
        for m in range(nm):
            for h in range(2):
                tile = nt(eye, array[h * BLOCK : (h + 1) * BLOCK, m * chunk : (m + 1) * chunk])
                rows = [
                    tile[y * nz + zh * ZLO : y * nz + (zh + 1) * ZLO]
                    for zh in range(ny_dev)
                    for y in range(YLO)
                ]
                into[m, h] = jnp.concatenate(rows, axis=0).astype(BF16)

    turn(prior, turned)
    pl.semaphore_wait(barrier, group - 1 + nz_dev - 1)

    local = pltpu.make_async_copy(turned.at[me_m], cur_a.at[me_m], s0_recv.at[0])
    local.start()
    for j in range(1, nm):
        m = (me_m + j) % nm
        remote(turned.at[m], cur_a.at[me_m], s0_send.at[0], s0_recv.at[0], (me_c, m)).start()
    pltpu.make_async_copy(coef_own, coef.at[me_m], s0_recv.at[2]).start()
    for j in range(1, nm):
        m = (me_m + j) % nm
        remote(coef_own, coef.at[me_m], s0_send.at[2], s0_recv.at[2], (me_c, m)).start()
    sibling = me_x * 2 + 1 - me_core
    for j in range(1, chips):
        x = (me_x + j) % chips
        remote(
            coupling, blocks.at[me_m], gather_send.at[0], gather_recv.at[j], (me_c, x * 2 + me_core)
        ).start()
    remote(coupling, blocks.at[me_m], gather_send.at[1], gather_recv.at[0], (me_c, sibling)).start()
    own_blocks = pltpu.make_async_copy(coupling, blocks.at[me_m], gather_send.at[3])
    own_blocks.start()
    turn(source, turned_s)
    pltpu.make_async_copy(turned_s.at[me_m], emission.at[me_m], s0_recv.at[1]).start()
    for j in range(1, nm):
        m = (me_m + j) % nm
        remote(turned_s.at[m], emission.at[me_m], s0_send.at[1], s0_recv.at[1], (me_c, m)).start()
    for j in range(1, chips):
        m = ((me_x + chips - j) % chips) * 2 + me_core
        await_bytes(blocks.at[m], gather_recv.at[j])
        remote(blocks.at[m], blocks.at[m], gather_send.at[2], gather_recv.at[0], (me_c, sibling)).start()
    own_blocks.wait()
    await_bytes(cur_a, s0_recv.at[0])
    await_bytes(coef, s0_recv.at[2])
    await_bytes(blocks.at[pl.ds(0, chips)], gather_recv.at[0])
    await_bytes(emission, s0_recv.at[1])

    for iteration in range(ITERS):
        current = cur_a if iteration == 0 else cur_b
        last = iteration == ITERS - 1

        def scatter(j, carry):
            m = (me_m + 1 + j) % nm
            for h in range(2):
                row = m * 2 + h
                left = jnp.concatenate([current[pairs[row, k] // 2, pairs[row, k] % 2] for k in range(PER_ROW)], axis=1)
                right = jnp.concatenate([blocks[m, h * PER_ROW + k] for k in range(PER_ROW)], axis=1)
                total = nt(left, right) + emission[m, h].astype(F32)
                for zh in range(ny_dev):
                    for y in range(YLO):
                        work[h * chunk + y * nz + zh * ZLO : h * chunk + y * nz + (zh + 1) * ZLO, :] = total[
                            (zh * YLO + y) * ZLO : (zh * YLO + y + 1) * ZLO
                        ]
            values = [work[pl.ds(z, 8, stride=nz), :] for z in range(nz)]
            values = run(values, coef[m, 0], coef[m, 1] > 0.5)
            largest = jnp.abs(values[0])
            for z in range(nz):
                work[pl.ds(z, 8, stride=nz), :] = values[z]
                if z:
                    largest = jnp.maximum(largest, jnp.abs(values[z]))
            largest = jnp.maximum(jnp.max(largest, axis=0, keepdims=True), 1e-30)
            xs_send[m] = largest * (1.0 / TOP)
            scale = TOP / largest
            for zh in range(ny_dev):
                for h in range(2):
                    for y in range(0, YLO, 2):
                        rows = [
                            work[h * chunk + (y + i) * nz + zh * ZLO : h * chunk + (y + i) * nz + (zh + 1) * ZLO, :]
                            for i in range(2)
                        ]
                        x_send[m * ny_dev + zh, h, y * ZLO : (y + 2) * ZLO, :] = encode(
                            jnp.concatenate(rows, axis=0), scale
                        )
            slot = me_m * ny_dev + me_y
            for i in range(ny_dev):
                y = (me_y + 1 + i) % ny_dev
                to = (me_z * ny_dev + y, m)

                def send():
                    remote(x_send.at[m * ny_dev + y], x_recv.at[slot], x_sem.at[0], x_sem.at[1], to).start()
                    remote(xs_send.at[m], xs_recv.at[slot], scale_sem.at[0], scale_sem.at[1], to).start()

                def keep():
                    pltpu.make_async_copy(x_send.at[m * ny_dev + y], x_recv.at[slot], x_sem.at[1]).start()
                    pltpu.make_async_copy(xs_send.at[m], xs_recv.at[slot], scale_sem.at[1]).start()

                if i < ny_dev - 1:
                    send()
                else:
                    pl.when(j < nm - 1)(send)
                    pl.when(j == nm - 1)(keep)
            return carry

        lax.fori_loop(0, nm, scatter, 0)
        await_bytes(x_recv, x_sem.at[1])
        await_bytes(xs_recv, scale_sem.at[1])

        def unpack(m, carry):
            for h in range(2):
                got = []
                for x in range(XLO):
                    factor = xs_recv[m * ny_dev + x] * weight[h]
                    value = decode(x_recv[m * ny_dev + x, h]) * factor
                    planes[h, x, pl.ds(m * YLO * ZLO, YLO * ZLO), :] = value
                    got.append(value)
                t = jnp.concatenate([fac[0, h]] * YLO, axis=0)
                f = jnp.concatenate([transmission_dir(h)] * YLO, axis=0) == 1
                end = jnp.where(f, got[0], got[XLO - 1])
                for x in range(1, XLO):
                    end = end * t + jnp.where(f, got[x], got[XLO - 1 - x])
                ends[h, pl.ds(m * YLO * ZLO, YLO * ZLO), :] = end
            return carry

        def transmission_dir(h):
            return jnp.broadcast_to(direction[0:1, h * BLOCK : (h + 1) * BLOCK], (8, BLOCK))

        lax.fori_loop(0, nm, unpack, 0)
        largest = jnp.full((8, BLOCK), 1e-30, F32)
        for h in range(2):
            values = [ends[h, y * ZLO : (y + 1) * ZLO, :] for y in range(ny)]
            values = run(values, fac[1, h], fwd[1, h])
            for y in range(ny):
                ends[h, y * ZLO : (y + 1) * ZLO, :] = values[y]
                largest = jnp.maximum(largest, jnp.abs(values[y]))
        largest = jnp.max(largest, axis=0, keepdims=True)
        es_send[...] = largest * (1.0 / TOP)
        scale = TOP / largest

        def send_ends(j, carry):
            z = (me_z + 1 + j) % nz_dev
            for h in range(2):
                e_send[z, h] = encode(ends[h, pl.ds(z * per_z, per_z), :], scale)
            to = (z * ny_dev + me_y, me_m)

            @pl.when(j < nz_dev - 1)
            def _():
                remote(e_send.at[z], e_recv.at[me_z], e_sem.at[0], e_sem.at[1], to).start()
                remote(es_send, es_recv.at[me_z], scale_sem.at[2], scale_sem.at[3], to).start()

            @pl.when(j == nz_dev - 1)
            def _():
                pltpu.make_async_copy(e_send.at[z], e_recv.at[me_z], e_sem.at[1]).start()
                pltpu.make_async_copy(es_send, es_recv.at[me_z], scale_sem.at[3]).start()

            return carry

        lax.fori_loop(0, nz_dev, send_ends, 0)

        def sweep_y(h):
            def one(x, carry):
                values = [planes[h, x, y * ZLO : (y + 1) * ZLO, :] for y in range(ny)]
                values = run(values, fac[1, h], fwd[1, h])
                for y in range(ny):
                    planes[h, x, y * ZLO : (y + 1) * ZLO, :] = values[y]
                return carry

            lax.fori_loop(0, XLO, one, 0)

        sweep_y(0)
        await_bytes(e_recv, e_sem.at[1])
        await_bytes(es_recv, scale_sem.at[3])

        largest = jnp.full((8, BLOCK), 1e-30, F32)
        for h in range(2):
            leap = fac[0, h] * fac[0, h]
            leap = leap * leap
            for part in range(per_z // 16):
                got = [
                    decode(e_recv[z, h, part * 16 : part * 16 + 16, :]) * es_recv[z] for z in range(nz_dev)
                ]
                for i in range(2):
                    f = fwd[0, h]
                    given = [g[i * 8 : i * 8 + 8] for g in got]
                    ordered = [jnp.where(f, given[s], given[nz_dev - 1 - s]) for s in range(nz_dev)]
                    taken = [jnp.zeros_like(ordered[0])]
                    for s in range(nz_dev - 1):
                        taken.append(leap * taken[-1] + ordered[s])
                    for z in range(nz_dev):
                        value = jnp.where(f, taken[z], taken[nz_dev - 1 - z])
                        ends[h, z * per_z + part * 16 + i * 8 : z * per_z + part * 16 + i * 8 + 8, :] = value
                        largest = jnp.maximum(largest, jnp.abs(value))
        largest = jnp.max(largest, axis=0, keepdims=True)
        bs_send[...] = largest * (1.0 / TOP)
        scale = TOP / largest

        def send_back(j, carry):
            z = (me_z + 1 + j) % nz_dev
            for h in range(2):
                b_send[z, h] = encode(ends[h, pl.ds(z * per_z, per_z), :], scale)
            to = (z * ny_dev + me_y, me_m)

            @pl.when(j < nz_dev - 1)
            def _():
                remote(b_send.at[z], b_recv.at[me_z], b_sem.at[0], b_sem.at[1], to).start()
                remote(bs_send, bs_recv.at[me_z], scale_sem.at[4], scale_sem.at[5], to).start()

            @pl.when(j == nz_dev - 1)
            def _():
                pltpu.make_async_copy(b_send.at[z], b_recv.at[me_z], b_sem.at[1]).start()
                pltpu.make_async_copy(bs_send, bs_recv.at[me_z], scale_sem.at[5]).start()

            return carry

        lax.fori_loop(0, nz_dev, send_back, 0)
        sweep_y(1)
        await_bytes(b_recv, b_sem.at[1])
        await_bytes(bs_recv, scale_sem.at[5])

        def inflow(z, carry):
            for h in range(2):
                ends[h, pl.ds(z * per_z, per_z), :] = decode(b_recv[z, h]) * bs_recv[z]
            return carry

        lax.fori_loop(0, nz_dev, inflow, 0)

        def finish(j, carry):
            m = (me_m + 1 + j) % nm
            rows = pl.ds(m * YLO * ZLO, YLO * ZLO)
            for h in range(2):
                t = jnp.concatenate([fac[0, h]] * YLO, axis=0)
                f = jnp.concatenate([transmission_dir(h)] * YLO, axis=0) == 1
                given = [planes[h, x, rows, :] for x in range(XLO)]
                value = ends[h, rows, :]
                swept = []
                for x in range(XLO):
                    value = t * value + jnp.where(f, given[x], given[XLO - 1 - x])
                    swept.append(value)
                for x in range(XLO):
                    result = jnp.where(f, swept[x], swept[XLO - 1 - x]).astype(BF16)
                    if last:
                        f_send[x, h, rows, :] = result
                    else:
                        c_send[m * ny_dev + x, h] = result
            if not last:
                for i in range(ny_dev):
                    y = (me_y + 1 + i) % ny_dev
                    to = (me_z * ny_dev + y, m)
                    into = cur_b.at[me_m, :, pl.ds(me_y * YLO * ZLO, YLO * ZLO), :]

                    def send():
                        remote(c_send.at[m * ny_dev + y], into, c_sem.at[0], c_sem.at[1], to).start()

                    def keep():
                        pltpu.make_async_copy(c_send.at[m * ny_dev + y], into, c_sem.at[1]).start()

                    if i < ny_dev - 1:
                        send()
                    else:
                        pl.when(j < nm - 1)(send)
                        pl.when(j == nm - 1)(keep)
            return carry

        lax.fori_loop(0, nm, finish, 0)
        await_bytes(x_send.at[pl.ds(0, group - 1)], x_sem.at[0])
        await_bytes(xs_recv.at[pl.ds(0, group - 1)], scale_sem.at[0])
        await_bytes(e_send.at[pl.ds(0, nz_dev - 1)], e_sem.at[0])
        await_bytes(es_recv.at[pl.ds(0, nz_dev - 1)], scale_sem.at[2])
        await_bytes(b_send.at[pl.ds(0, nz_dev - 1)], b_sem.at[0])
        await_bytes(bs_recv.at[pl.ds(0, nz_dev - 1)], scale_sem.at[4])
        if not last:
            await_bytes(cur_b, c_sem.at[1])
            await_bytes(c_send.at[pl.ds(0, group - 1)], c_sem.at[0])

    for i in range(1, ny_dev):
        y = (me_y + i) % ny_dev
        remote(f_send.at[y], f_recv.at[me_y], f_sem.at[0], f_sem.at[1], (me_z * ny_dev + y, me_m)).start()
    pltpu.make_async_copy(f_send.at[me_y], f_recv.at[me_y], f_sem.at[1]).start()
    await_bytes(turned.at[pl.ds(0, nm - 1)], s0_send.at[0])
    await_bytes(turned_s.at[pl.ds(0, nm - 1)], s0_send.at[1])
    await_bytes(coef.at[pl.ds(0, nm - 1)], s0_send.at[2])
    if chips > 1:
        await_bytes(blocks.at[pl.ds(0, chips - 1)], gather_send.at[0])
        await_bytes(blocks.at[pl.ds(0, chips - 1)], gather_send.at[2])
    await_bytes(coupling, gather_send.at[1])
    await_bytes(f_recv, f_sem.at[1])
    wide = identity(BLOCK)
    for m in range(nm):
        for h in range(2):
            parts = []
            for zh in range(ny_dev):
                parts.append(f_recv[zh, h, m * YLO * ZLO : (m + 1) * YLO * ZLO, :].astype(F32))
            rows = [parts[zh][y * ZLO : (y + 1) * ZLO] for y in range(YLO) for zh in range(ny_dev)]
            tile = jnp.concatenate(rows, axis=0).astype(BF16)
            out[h * BLOCK : (h + 1) * BLOCK, m * chunk : (m + 1) * chunk] = nt(wide, tile).astype(BF16)
    await_bytes(f_send.at[pl.ds(0, ny_dev - 1)], f_sem.at[0])


def local(dims, source, prior, coupling, pairs, transmission, direction):
    nm, ny_dev, nz_dev, ny, nz = dims
    modes = source.shape[0]
    group = nm * ny_dev
    chunk = YLO * nz
    tall = ny * ZLO
    per_z = tall // nz_dev
    vmem = pl.BlockSpec(memory_space=pltpu.VMEM)
    dma = pltpu.SemaphoreType.DMA
    result = pl.pallas_call(
        functools.partial(kernel, dims),
        out_shape=jax.ShapeDtypeStruct((modes, ny * nz), BF16),
        in_specs=[vmem, vmem, vmem, pl.BlockSpec(memory_space=pltpu.SMEM), vmem, vmem],
        out_specs=vmem,
        scratch_shapes=[
            pltpu.VMEM((nm, 2, chunk, BLOCK), BF16),
            pltpu.VMEM((nm, 2, chunk, BLOCK), BF16),
            pltpu.VMEM((nm, 2, chunk, BLOCK), BF16),
            pltpu.VMEM((nm, 2, chunk, BLOCK), BF16),
            pltpu.VMEM((nm, 2, chunk, BLOCK), BF16),
            pltpu.VMEM((nm, 2 * PER_ROW, BLOCK, BLOCK), BF16),
            pltpu.VMEM((2, 8, BLOCK), F32),
            pltpu.VMEM((nm, 2, 8, BLOCK), F32),
            pltpu.VMEM((2 * chunk, BLOCK), F32),
            pltpu.VMEM((group, 2, YLO * ZLO, BLOCK), I16),
            pltpu.VMEM((group, 2, YLO * ZLO, BLOCK), I16),
            pltpu.VMEM((nm, 1, BLOCK), F32),
            pltpu.VMEM((group, 1, BLOCK), F32),
            pltpu.VMEM((2, XLO, tall, BLOCK), F32),
            pltpu.VMEM((2, tall, BLOCK), F32),
            pltpu.VMEM((nz_dev, 2, per_z, BLOCK), I16),
            pltpu.VMEM((nz_dev, 2, per_z, BLOCK), I16),
            pltpu.VMEM((1, BLOCK), F32),
            pltpu.VMEM((nz_dev, 1, BLOCK), F32),
            pltpu.VMEM((nz_dev, 2, per_z, BLOCK), I16),
            pltpu.VMEM((nz_dev, 2, per_z, BLOCK), I16),
            pltpu.VMEM((1, BLOCK), F32),
            pltpu.VMEM((nz_dev, 1, BLOCK), F32),
            pltpu.VMEM((group, 2, YLO * ZLO, BLOCK), BF16),
            pltpu.VMEM((ny_dev, 2, tall, BLOCK), BF16),
            pltpu.VMEM((ny_dev, 2, tall, BLOCK), BF16),
            dma((3,)),
            dma((3,)),
            dma((4,)),
            dma((nm // 2,)),
            dma((2,)),
            dma((2,)),
            dma((2,)),
            dma((2,)),
            dma((2,)),
            dma((6,)),
        ],
        compiler_params=pltpu.CompilerParams(
            collective_id=0, has_side_effects=True, vmem_limit_bytes=40 * 1024 * 1024
        ),
        cost_estimate=pl.CostEstimate(flops=600_000_000, bytes_accessed=2_000_000, transcendentals=0),
    )(
        source.reshape(modes, ny * nz),
        prior.reshape(modes, ny * nz),
        coupling.reshape(2 * PER_ROW, BLOCK, BLOCK),
        pairs,
        transmission,
        direction,
    )
    return result.reshape(modes, 1, ny * nz)


def build(mesh, ny, nz):
    nm = mesh.shape["mode"]
    ny_dev = nz // ZLO
    nz_dev = mesh.shape["cell"] // ny_dev
    in_specs = (
        P("mode", "cell", None),
        P("mode", "cell", None),
        P("mode", None, None, None),
        P(),
        P(None, "mode"),
        P(None, "mode"),
    )
    body = functools.partial(local, (nm, ny_dev, nz_dev, ny, nz))
    return jax.shard_map(body, mesh=mesh, in_specs=in_specs, out_specs=P("mode", "cell", None), check_vma=False)


def solution(mesh):
    return build(mesh, 32, 32)
```

```python
import functools

import jax
import jax.numpy as jnp
from jax import lax
from jax.experimental import pallas as pl
from jax.experimental.pallas import tpu as pltpu
from jax.sharding import PartitionSpec as P

ITERS = 2
BLOCK = 128
PER_ROW = 4
ZLO = 8
YLO = 4
XLO = 4
TOP = 32767.0
F32 = jnp.float32
BF16 = jnp.bfloat16
I16 = jnp.int16
MESH = pl.DeviceIdType.MESH


def nt(left, right):
    return lax.dot_general(left, right, (((1,), (1,)), ((), ())), preferred_element_type=F32)


def identity(size):
    rows = lax.broadcasted_iota(jnp.int32, (size, size), 0)
    columns = lax.broadcasted_iota(jnp.int32, (size, size), 1)
    return jnp.where(rows == columns, 1.0, 0.0).astype(BF16)


def run(values, factor, forward):
    n = len(values)
    ordered = [jnp.where(forward, values[s], values[n - 1 - s]) for s in range(n)]
    swept = [ordered[0]]
    for s in range(1, n):
        swept.append(factor * swept[-1] + ordered[s])
    return [jnp.where(forward, swept[s], swept[n - 1 - s]) for s in range(n)]


def encode(values, scale):
    return jnp.round(values * scale).astype(jnp.int32).astype(I16)


def decode(codes):
    return codes.astype(jnp.int32).astype(F32)


def kernel(
    dims,
    source,
    prior,
    coupling,
    pairs,
    transmission,
    direction,
    out,
    source_v,
    prior_v,
    cur_a,
    cur_b,
    turned,
    s_send,
    s_recv,
    ss_send,
    ss_recv,
    blocks,
    coef_own,
    coef,
    work,
    x_send,
    x_recv,
    xs_send,
    xs_recv,
    planes,
    ends,
    e_send,
    e_recv,
    es_send,
    es_recv,
    b_send,
    b_recv,
    bs_send,
    bs_recv,
    c_send,
    f_send,
    f_recv,
    in_sem,
    s0_send,
    s0_recv,
    gather_send,
    gather_recv,
    direct_sem,
    part_sem,
    x_sem,
    e_sem,
    b_sem,
    c_sem,
    f_sem,
    scale_sem,
):
    nm, ny_dev, nz_dev, ny, nz = dims
    chips = nm // 2
    chunk = YLO * nz
    tall = ny * ZLO
    per_z = tall // nz_dev
    me_m = lax.axis_index("mode")
    me_c = lax.axis_index("cell")
    me_z, me_y = me_c // ny_dev, me_c % ny_dev
    me_x, me_core = me_m // 2, me_m % 2

    def remote(src, dst, send, recv, to):
        return pltpu.make_async_remote_copy(
            src_ref=src, dst_ref=dst, send_sem=send, recv_sem=recv, device_id=to, device_id_type=MESH
        )

    def await_bytes(ref, sem):
        pltpu.make_async_copy(ref, ref, sem).wait()

    loads = [
        pltpu.make_async_copy(prior, prior_v, in_sem.at[0]),
        pltpu.make_async_copy(coupling, blocks.at[me_m], in_sem.at[1]),
        pltpu.make_async_copy(source, source_v, in_sem.at[2]),
    ]
    for load in loads:
        load.start()

    barrier = pltpu.get_barrier_semaphore()
    group = nm * ny_dev
    far = nz_dev // 2

    def greet_ring(j, carry):
        step = far + jnp.where(j % 2 == 0, j // 2, -(j + 1) // 2)
        z = (me_z + step) % nz_dev
        pl.semaphore_signal(barrier, inc=1, device_id=(z * ny_dev + me_y, me_m), device_id_type=MESH)
        return carry

    lax.fori_loop(0, nz_dev - 1, greet_ring, 0)

    def greet_group(j, carry):
        m = (me_m + j // ny_dev) % nm
        y = (me_y + j % ny_dev) % ny_dev
        pl.semaphore_signal(barrier, inc=1, device_id=(me_z * ny_dev + y, m), device_id_type=MESH)
        return carry

    lax.fori_loop(1, group, greet_group, 0)

    fwd = {}
    fac = {}
    weight = {}
    for h in range(2):
        lanes = slice(h * BLOCK, (h + 1) * BLOCK)
        for d in range(3):
            fac[d, h] = jnp.broadcast_to(transmission[d : d + 1, lanes], (8, BLOCK))
            fwd[d, h] = jnp.broadcast_to(direction[d : d + 1, lanes], (8, BLOCK)) == 1
        total = jnp.sqrt(1.0 - transmission[0:1, lanes] * transmission[0:1, lanes])
        for d in range(1, 3):
            total = total * jnp.sqrt(1.0 - transmission[d : d + 1, lanes] * transmission[d : d + 1, lanes])
        weight[h] = total
    for h in range(2):
        coef_own[0, h * 4 : h * 4 + 4, :] = fac[2, h][:4]
        coef_own[1, h * 4 : h * 4 + 4, :] = jnp.where(fwd[2, h], 1.0, 0.0)[:4]

    eye = identity(chunk)

    loads[0].wait()
    for m in range(nm):
        for h in range(2):
            tile = nt(eye, prior_v[h * BLOCK : (h + 1) * BLOCK, m * chunk : (m + 1) * chunk])
            rows = [
                tile[y * nz + zh * ZLO : y * nz + (zh + 1) * ZLO] for zh in range(ny_dev) for y in range(YLO)
            ]
            turned[m, h] = jnp.concatenate(rows, axis=0).astype(BF16)

    def sweep_z(factor, forward):
        values = run([work[pl.ds(z, 8, stride=nz), :] for z in range(nz)], factor, forward)
        largest = jnp.abs(values[0])
        for z in range(nz):
            work[pl.ds(z, 8, stride=nz), :] = values[z]
            if z:
                largest = jnp.maximum(largest, jnp.abs(values[z]))
        largest = jnp.maximum(jnp.max(largest, axis=0, keepdims=True), 1e-30)
        return TOP / largest, largest * (1.0 / TOP)

    def two_rows(h, y, zh):
        start = h * chunk + y * nz + zh * ZLO
        return jnp.concatenate([work[start : start + ZLO, :], work[start + nz : start + nz + ZLO, :]], axis=0)

    loads[1].wait()
    pl.semaphore_wait(barrier, group - 1 + nz_dev - 1)

    sibling = me_x * 2 + 1 - me_core
    shared = pl.ds(PER_ROW + me_y, 1)
    direct = pl.ds(0, PER_ROW)
    for j in range(1, chips):
        to = (me_c, ((me_x + j) % chips) * 2 + me_core)
        part = blocks.at[me_m, shared]
        remote(part, part, gather_send.at[0], part_sem.at[j], to).start()
    pltpu.make_async_copy(turned.at[me_m], cur_a.at[me_m], s0_recv.at[0]).start()
    for j in range(1, nm):
        m = (me_m + j) % nm
        remote(turned.at[m], cur_a.at[me_m], s0_send.at[0], s0_recv.at[0], (me_c, m)).start()
    pltpu.make_async_copy(coef_own, coef.at[me_m], s0_recv.at[2]).start()
    for j in range(1, nm):
        m = (me_m + j) % nm
        remote(coef_own, coef.at[me_m], s0_send.at[2], s0_recv.at[2], (me_c, m)).start()
    for j in range(1, chips):
        to = (me_c, ((me_x + j) % chips) * 2 + me_core)
        part = blocks.at[me_m, direct]
        remote(part, part, gather_send.at[1], direct_sem.at[j], to).start()
    own = blocks.at[me_m]
    remote(own, own, gather_send.at[2], gather_recv.at[1], (me_c, sibling)).start()

    def over_y(m):
        part = blocks.at[m, shared]
        for i in range(1, ny_dev):
            to = (me_z * ny_dev + (me_y + i) % ny_dev, me_m)
            remote(part, part, gather_send.at[3], gather_recv.at[0], to).start()

    for j in range(1, chips):
        m = ((me_x + chips - j) % chips) * 2 + me_core
        await_bytes(blocks.at[m, shared], part_sem.at[j])
        over_y(m)

    loads[2].wait()

    def sweep_source(m, carry):
        for h in range(2):
            columns = pl.ds(pl.multiple_of(m * chunk, chunk), chunk)
            work[h * chunk : (h + 1) * chunk, :] = nt(eye, source_v[h * BLOCK : (h + 1) * BLOCK, columns])
        scale, unit = sweep_z(coef_own[0], coef_own[1] > 0.5)
        ss_send[m] = unit
        for zh in range(ny_dev):
            for h in range(2):
                for y in range(0, YLO, 2):
                    rows = pl.ds(m * YLO * ZLO + y * ZLO, 2 * ZLO)
                    s_send[zh, h, rows, :] = encode(two_rows(h, y, zh), scale)
        return carry

    lax.fori_loop(0, nm, sweep_source, 0)
    for i in range(1, ny_dev):
        y = (me_y + i) % ny_dev
        to = (me_z * ny_dev + y, me_m)
        remote(s_send.at[y], s_recv.at[me_y], s0_send.at[1], s0_recv.at[1], to).start()
        remote(ss_send, ss_recv.at[me_y], s0_send.at[3], s0_recv.at[3], to).start()
    pltpu.make_async_copy(s_send.at[me_y], s_recv.at[me_y], s0_recv.at[1]).start()
    pltpu.make_async_copy(ss_send, ss_recv.at[me_y], s0_recv.at[3]).start()
    for j in range(1, chips):
        part = blocks.at[((me_x + chips - j) % chips) * 2 + me_core, direct]
        await_bytes(part, direct_sem.at[j])
        remote(part, part, gather_send.at[4], gather_recv.at[1], (me_c, sibling)).start()
    if chips > 1:
        await_bytes(blocks.at[pl.ds(0, chips - 1), pl.ds(0, ny_dev - 1)], gather_recv.at[0])
    for j in range(1, chips):
        part = blocks.at[((me_x + chips - j) % chips) * 2 + me_core, pl.ds(PER_ROW, PER_ROW)]
        remote(part, part, gather_send.at[4], gather_recv.at[1], (me_c, sibling)).start()
    await_bytes(cur_a, s0_recv.at[0])
    await_bytes(coef, s0_recv.at[2])
    await_bytes(blocks.at[pl.ds(0, chips)], gather_recv.at[1])

    for iteration in range(ITERS):
        current = cur_a if iteration == 0 else cur_b
        last = iteration == ITERS - 1

        def scatter(j, carry):
            m = (me_m + 1 + j) % nm
            for h in range(2):
                row = m * 2 + h
                left = jnp.concatenate([current[pairs[row, k] // 2, pairs[row, k] % 2] for k in range(PER_ROW)], axis=1)
                right = jnp.concatenate([blocks[m, h * PER_ROW + k] for k in range(PER_ROW)], axis=1)
                total = nt(left, right)
                for zh in range(ny_dev):
                    for y in range(YLO):
                        work[h * chunk + y * nz + zh * ZLO : h * chunk + y * nz + (zh + 1) * ZLO, :] = total[
                            (zh * YLO + y) * ZLO : (zh * YLO + y + 1) * ZLO
                        ]
            scale, unit = sweep_z(coef[m, 0], coef[m, 1] > 0.5)
            xs_send[m] = unit
            for zh in range(ny_dev):
                for h in range(2):
                    for y in range(0, YLO, 2):
                        x_send[m * ny_dev + zh, h, y * ZLO : (y + 2) * ZLO, :] = encode(two_rows(h, y, zh), scale)
            slot = me_m * ny_dev + me_y
            for i in range(ny_dev):
                y = (me_y + 1 + i) % ny_dev
                to = (me_z * ny_dev + y, m)

                def send():
                    remote(x_send.at[m * ny_dev + y], x_recv.at[slot], x_sem.at[0], x_sem.at[1], to).start()
                    remote(xs_send.at[m], xs_recv.at[slot], scale_sem.at[0], scale_sem.at[1], to).start()

                def keep():
                    pltpu.make_async_copy(x_send.at[m * ny_dev + y], x_recv.at[slot], x_sem.at[1]).start()
                    pltpu.make_async_copy(xs_send.at[m], xs_recv.at[slot], scale_sem.at[1]).start()

                if i < ny_dev - 1:
                    send()
                else:
                    pl.when(j < nm - 1)(send)
                    pl.when(j == nm - 1)(keep)
            return carry

        lax.fori_loop(0, nm, scatter, 0)
        await_bytes(x_recv, x_sem.at[1])
        await_bytes(xs_recv, scale_sem.at[1])
        if iteration == 0:
            await_bytes(s_recv, s0_recv.at[1])
            await_bytes(ss_recv, s0_recv.at[3])

        def unpack(m, carry):
            for h in range(2):
                got = []
                for x in range(XLO):
                    rows = pl.ds(m * YLO * ZLO, YLO * ZLO)
                    value = decode(x_recv[m * ny_dev + x, h]) * (xs_recv[m * ny_dev + x] * weight[h])
                    value += decode(s_recv[x, h, rows, :]) * (ss_recv[x, m] * weight[h])
                    planes[h, x, rows, :] = value
                    got.append(value)
                t = jnp.concatenate([fac[0, h]] * YLO, axis=0)
                f = jnp.concatenate([transmission_dir(h)] * YLO, axis=0) == 1
                end = jnp.where(f, got[0], got[XLO - 1])
                for x in range(1, XLO):
                    end = end * t + jnp.where(f, got[x], got[XLO - 1 - x])
                ends[h, pl.ds(m * YLO * ZLO, YLO * ZLO), :] = end
            return carry

        def transmission_dir(h):
            return jnp.broadcast_to(direction[0:1, h * BLOCK : (h + 1) * BLOCK], (8, BLOCK))

        lax.fori_loop(0, nm, unpack, 0)
        largest = jnp.full((8, BLOCK), 1e-30, F32)
        for h in range(2):
            values = [ends[h, y * ZLO : (y + 1) * ZLO, :] for y in range(ny)]
            values = run(values, fac[1, h], fwd[1, h])
            for y in range(ny):
                ends[h, y * ZLO : (y + 1) * ZLO, :] = values[y]
                largest = jnp.maximum(largest, jnp.abs(values[y]))
        largest = jnp.max(largest, axis=0, keepdims=True)
        es_send[...] = largest * (1.0 / TOP)
        scale = TOP / largest

        def send_ends(j, carry):
            z = (me_z + 1 + j) % nz_dev
            for h in range(2):
                e_send[z, h] = encode(ends[h, pl.ds(z * per_z, per_z), :], scale)
            to = (z * ny_dev + me_y, me_m)

            @pl.when(j < nz_dev - 1)
            def _():
                remote(e_send.at[z], e_recv.at[me_z], e_sem.at[0], e_sem.at[1], to).start()
                remote(es_send, es_recv.at[me_z], scale_sem.at[2], scale_sem.at[3], to).start()

            @pl.when(j == nz_dev - 1)
            def _():
                pltpu.make_async_copy(e_send.at[z], e_recv.at[me_z], e_sem.at[1]).start()
                pltpu.make_async_copy(es_send, es_recv.at[me_z], scale_sem.at[3]).start()

            return carry

        lax.fori_loop(0, nz_dev, send_ends, 0)

        def sweep_y(h):
            def one(x, carry):
                values = [planes[h, x, y * ZLO : (y + 1) * ZLO, :] for y in range(ny)]
                values = run(values, fac[1, h], fwd[1, h])
                for y in range(ny):
                    planes[h, x, y * ZLO : (y + 1) * ZLO, :] = values[y]
                return carry

            lax.fori_loop(0, XLO, one, 0)

        sweep_y(0)
        await_bytes(e_recv, e_sem.at[1])
        await_bytes(es_recv, scale_sem.at[3])

        largest = jnp.full((8, BLOCK), 1e-30, F32)
        for h in range(2):
            leap = fac[0, h] * fac[0, h]
            leap = leap * leap
            for part in range(per_z // 16):
                got = [
                    decode(e_recv[z, h, part * 16 : part * 16 + 16, :]) * es_recv[z] for z in range(nz_dev)
                ]
                for i in range(2):
                    f = fwd[0, h]
                    given = [g[i * 8 : i * 8 + 8] for g in got]
                    ordered = [jnp.where(f, given[s], given[nz_dev - 1 - s]) for s in range(nz_dev)]
                    taken = [jnp.zeros_like(ordered[0])]
                    for s in range(nz_dev - 1):
                        taken.append(leap * taken[-1] + ordered[s])
                    for z in range(nz_dev):
                        value = jnp.where(f, taken[z], taken[nz_dev - 1 - z])
                        ends[h, z * per_z + part * 16 + i * 8 : z * per_z + part * 16 + i * 8 + 8, :] = value
                        largest = jnp.maximum(largest, jnp.abs(value))
        largest = jnp.max(largest, axis=0, keepdims=True)
        bs_send[...] = largest * (1.0 / TOP)
        scale = TOP / largest

        def send_back(j, carry):
            z = (me_z + 1 + j) % nz_dev
            for h in range(2):
                b_send[z, h] = encode(ends[h, pl.ds(z * per_z, per_z), :], scale)
            to = (z * ny_dev + me_y, me_m)

            @pl.when(j < nz_dev - 1)
            def _():
                remote(b_send.at[z], b_recv.at[me_z], b_sem.at[0], b_sem.at[1], to).start()
                remote(bs_send, bs_recv.at[me_z], scale_sem.at[4], scale_sem.at[5], to).start()

            @pl.when(j == nz_dev - 1)
            def _():
                pltpu.make_async_copy(b_send.at[z], b_recv.at[me_z], b_sem.at[1]).start()
                pltpu.make_async_copy(bs_send, bs_recv.at[me_z], scale_sem.at[5]).start()

            return carry

        lax.fori_loop(0, nz_dev, send_back, 0)
        sweep_y(1)
        await_bytes(b_recv, b_sem.at[1])
        await_bytes(bs_recv, scale_sem.at[5])

        def inflow(z, carry):
            for h in range(2):
                ends[h, pl.ds(z * per_z, per_z), :] = decode(b_recv[z, h]) * bs_recv[z]
            return carry

        lax.fori_loop(0, nz_dev, inflow, 0)

        def finish(j, carry):
            m = (me_m + 1 + j) % nm
            rows = pl.ds(m * YLO * ZLO, YLO * ZLO)
            for h in range(2):
                t = jnp.concatenate([fac[0, h]] * YLO, axis=0)
                f = jnp.concatenate([transmission_dir(h)] * YLO, axis=0) == 1
                given = [planes[h, x, rows, :] for x in range(XLO)]
                value = ends[h, rows, :]
                swept = []
                for x in range(XLO):
                    value = t * value + jnp.where(f, given[x], given[XLO - 1 - x])
                    swept.append(value)
                for x in range(XLO):
                    result = jnp.where(f, swept[x], swept[XLO - 1 - x]).astype(BF16)
                    if last:
                        f_send[x, h, rows, :] = result
                    else:
                        c_send[m * ny_dev + x, h] = result
            if not last:
                for i in range(ny_dev):
                    y = (me_y + 1 + i) % ny_dev
                    to = (me_z * ny_dev + y, m)
                    into = cur_b.at[me_m, :, pl.ds(me_y * YLO * ZLO, YLO * ZLO), :]

                    def send():
                        remote(c_send.at[m * ny_dev + y], into, c_sem.at[0], c_sem.at[1], to).start()

                    def keep():
                        pltpu.make_async_copy(c_send.at[m * ny_dev + y], into, c_sem.at[1]).start()

                    if i < ny_dev - 1:
                        send()
                    else:
                        pl.when(j < nm - 1)(send)
                        pl.when(j == nm - 1)(keep)
            return carry

        lax.fori_loop(0, nm, finish, 0)
        await_bytes(x_send.at[pl.ds(0, group - 1)], x_sem.at[0])
        await_bytes(xs_recv.at[pl.ds(0, group - 1)], scale_sem.at[0])
        await_bytes(e_send.at[pl.ds(0, nz_dev - 1)], e_sem.at[0])
        await_bytes(es_recv.at[pl.ds(0, nz_dev - 1)], scale_sem.at[2])
        await_bytes(b_send.at[pl.ds(0, nz_dev - 1)], b_sem.at[0])
        await_bytes(bs_recv.at[pl.ds(0, nz_dev - 1)], scale_sem.at[4])
        if not last:
            await_bytes(cur_b, c_sem.at[1])
            await_bytes(c_send.at[pl.ds(0, group - 1)], c_sem.at[0])

    for i in range(1, ny_dev):
        y = (me_y + i) % ny_dev
        remote(f_send.at[y], f_recv.at[me_y], f_sem.at[0], f_sem.at[1], (me_z * ny_dev + y, me_m)).start()
    pltpu.make_async_copy(f_send.at[me_y], f_recv.at[me_y], f_sem.at[1]).start()
    await_bytes(turned.at[pl.ds(0, nm - 1)], s0_send.at[0])
    await_bytes(s_send.at[pl.ds(0, ny_dev - 1)], s0_send.at[1])
    await_bytes(ss_recv.at[pl.ds(0, ny_dev - 1)], s0_send.at[3])
    await_bytes(coef.at[pl.ds(0, nm - 1)], s0_send.at[2])
    if chips > 1:
        await_bytes(blocks.at[0, pl.ds(0, chips - 1)], gather_send.at[0])
        await_bytes(blocks.at[pl.ds(0, chips - 1), direct], gather_send.at[1])
        await_bytes(blocks.at[pl.ds(0, chips - 1), pl.ds(0, ny_dev - 1)], gather_send.at[3])
        await_bytes(blocks.at[pl.ds(0, chips - 1)], gather_send.at[4])
    await_bytes(blocks.at[0], gather_send.at[2])
    await_bytes(f_recv, f_sem.at[1])
    wide = identity(BLOCK)
    for m in range(nm):
        for h in range(2):
            parts = []
            for zh in range(ny_dev):
                parts.append(f_recv[zh, h, m * YLO * ZLO : (m + 1) * YLO * ZLO, :].astype(F32))
            rows = [parts[zh][y * ZLO : (y + 1) * ZLO] for y in range(YLO) for zh in range(ny_dev)]
            tile = jnp.concatenate(rows, axis=0).astype(BF16)
            out[h * BLOCK : (h + 1) * BLOCK, m * chunk : (m + 1) * chunk] = nt(wide, tile).astype(BF16)
    await_bytes(f_send.at[pl.ds(0, ny_dev - 1)], f_sem.at[0])


def local(dims, source, prior, coupling, pairs, transmission, direction):
    nm, ny_dev, nz_dev, ny, nz = dims
    modes = source.shape[0]
    group = nm * ny_dev
    chunk = YLO * nz
    tall = ny * ZLO
    per_z = tall // nz_dev
    vmem = pl.BlockSpec(memory_space=pltpu.VMEM)
    hbm = pl.BlockSpec(memory_space=pl.ANY)
    dma = pltpu.SemaphoreType.DMA
    result = pl.pallas_call(
        functools.partial(kernel, dims),
        out_shape=jax.ShapeDtypeStruct((modes, ny * nz), BF16),
        in_specs=[hbm, hbm, hbm, pl.BlockSpec(memory_space=pltpu.SMEM), vmem, vmem],
        out_specs=vmem,
        scratch_shapes=[
            pltpu.VMEM((modes, ny * nz), BF16),
            pltpu.VMEM((modes, ny * nz), BF16),
            pltpu.VMEM((nm, 2, chunk, BLOCK), BF16),
            pltpu.VMEM((nm, 2, chunk, BLOCK), BF16),
            pltpu.VMEM((nm, 2, chunk, BLOCK), BF16),
            pltpu.VMEM((ny_dev, 2, tall, BLOCK), I16),
            pltpu.VMEM((ny_dev, 2, tall, BLOCK), I16),
            pltpu.VMEM((nm, 1, BLOCK), F32),
            pltpu.VMEM((ny_dev, nm, 1, BLOCK), F32),
            pltpu.VMEM((nm, 2 * PER_ROW, BLOCK, BLOCK), BF16),
            pltpu.VMEM((2, 8, BLOCK), F32),
            pltpu.VMEM((nm, 2, 8, BLOCK), F32),
            pltpu.VMEM((2 * chunk, BLOCK), F32),
            pltpu.VMEM((group, 2, YLO * ZLO, BLOCK), I16),
            pltpu.VMEM((group, 2, YLO * ZLO, BLOCK), I16),
            pltpu.VMEM((nm, 1, BLOCK), F32),
            pltpu.VMEM((group, 1, BLOCK), F32),
            pltpu.VMEM((2, XLO, tall, BLOCK), F32),
            pltpu.VMEM((2, tall, BLOCK), F32),
            pltpu.VMEM((nz_dev, 2, per_z, BLOCK), I16),
            pltpu.VMEM((nz_dev, 2, per_z, BLOCK), I16),
            pltpu.VMEM((1, BLOCK), F32),
            pltpu.VMEM((nz_dev, 1, BLOCK), F32),
            pltpu.VMEM((nz_dev, 2, per_z, BLOCK), I16),
            pltpu.VMEM((nz_dev, 2, per_z, BLOCK), I16),
            pltpu.VMEM((1, BLOCK), F32),
            pltpu.VMEM((nz_dev, 1, BLOCK), F32),
            pltpu.VMEM((group, 2, YLO * ZLO, BLOCK), BF16),
            pltpu.VMEM((ny_dev, 2, tall, BLOCK), BF16),
            pltpu.VMEM((ny_dev, 2, tall, BLOCK), BF16),
            dma((3,)),
            dma((4,)),
            dma((4,)),
            dma((5,)),
            dma((2,)),
            dma((nm // 2,)),
            dma((nm // 2,)),
            dma((2,)),
            dma((2,)),
            dma((2,)),
            dma((2,)),
            dma((2,)),
            dma((6,)),
        ],
        compiler_params=pltpu.CompilerParams(
            collective_id=0, has_side_effects=True, vmem_limit_bytes=40 * 1024 * 1024
        ),
        cost_estimate=pl.CostEstimate(flops=600_000_000, bytes_accessed=2_000_000, transcendentals=0),
    )(
        source.reshape(modes, ny * nz),
        prior.reshape(modes, ny * nz),
        coupling.reshape(2 * PER_ROW, BLOCK, BLOCK),
        pairs,
        transmission,
        direction,
    )
    return result.reshape(modes, 1, ny * nz)


def build(mesh, ny, nz):
    nm = mesh.shape["mode"]
    ny_dev = nz // ZLO
    nz_dev = mesh.shape["cell"] // ny_dev
    in_specs = (
        P("mode", "cell", None),
        P("mode", "cell", None),
        P("mode", None, None, None),
        P(),
        P(None, "mode"),
        P(None, "mode"),
    )
    body = functools.partial(local, (nm, ny_dev, nz_dev, ny, nz))
    return jax.shard_map(body, mesh=mesh, in_specs=in_specs, out_specs=P("mode", "cell", None), check_vma=False)


def solution(mesh):
    return build(mesh, 32, 32)
```

```python
import functools

import jax
import jax.numpy as jnp
from jax import lax
from jax.experimental import pallas as pl
from jax.experimental.pallas import tpu as pltpu
from jax.sharding import PartitionSpec as P

ITERS = 2
BLOCK = 128
PER_ROW = 4
ZLO = 8
YLO = 4
XLO = 4
TOP = 32767.0
F32 = jnp.float32
BF16 = jnp.bfloat16
I16 = jnp.int16
MESH = pl.DeviceIdType.MESH


def nt(left, right):
    return lax.dot_general(left, right, (((1,), (1,)), ((), ())), preferred_element_type=F32)


def identity(size):
    rows = lax.broadcasted_iota(jnp.int32, (size, size), 0)
    columns = lax.broadcasted_iota(jnp.int32, (size, size), 1)
    return jnp.where(rows == columns, 1.0, 0.0).astype(BF16)


def run(values, factor, forward):
    n = len(values)
    ordered = [jnp.where(forward, values[s], values[n - 1 - s]) for s in range(n)]
    swept = [ordered[0]]
    for s in range(1, n):
        swept.append(factor * swept[-1] + ordered[s])
    return [jnp.where(forward, swept[s], swept[n - 1 - s]) for s in range(n)]


def encode(values, scale):
    return jnp.round(values * scale).astype(jnp.int32).astype(I16)


def decode(codes):
    return codes.astype(jnp.int32).astype(F32)


def kernel(
    dims,
    source,
    prior,
    coupling,
    pairs,
    transmission,
    direction,
    out,
    source_v,
    prior_v,
    cur_a,
    cur_b,
    turned,
    s_send,
    s_recv,
    ss_send,
    ss_recv,
    blocks,
    coef_own,
    coef,
    work,
    x_send,
    x_recv,
    xs_send,
    xs_recv,
    planes,
    ends,
    e_send,
    e_recv,
    es_send,
    es_recv,
    b_send,
    b_recv,
    bs_send,
    bs_recv,
    c_send,
    f_send,
    f_recv,
    in_sem,
    s0_send,
    s0_recv,
    gather_send,
    gather_recv,
    direct_sem,
    part_sem,
    x_sem,
    e_sem,
    b_sem,
    c_sem,
    f_sem,
    scale_sem,
):
    nm, ny_dev, nz_dev, ny, nz = dims
    chips = nm // 2
    chunk = YLO * nz
    tall = ny * ZLO
    per_z = tall // nz_dev
    me_m = lax.axis_index("mode")
    me_c = lax.axis_index("cell")
    me_z, me_y = me_c // ny_dev, me_c % ny_dev
    me_x, me_core = me_m // 2, me_m % 2

    def remote(src, dst, send, recv, to):
        return pltpu.make_async_remote_copy(
            src_ref=src, dst_ref=dst, send_sem=send, recv_sem=recv, device_id=to, device_id_type=MESH
        )

    def await_bytes(ref, sem):
        pltpu.make_async_copy(ref, ref, sem).wait()

    loads = [
        pltpu.make_async_copy(prior, prior_v, in_sem.at[0]),
        pltpu.make_async_copy(coupling, blocks.at[me_m], in_sem.at[1]),
        pltpu.make_async_copy(source, source_v, in_sem.at[2]),
    ]
    for load in loads:
        load.start()

    barrier = pltpu.get_barrier_semaphore()
    group = nm * ny_dev
    far = nz_dev // 2

    def greet_ring(j, carry):
        step = far + jnp.where(j % 2 == 0, j // 2, -(j + 1) // 2)
        z = (me_z + step) % nz_dev
        pl.semaphore_signal(barrier, inc=1, device_id=(z * ny_dev + me_y, me_m), device_id_type=MESH)
        return carry

    lax.fori_loop(0, nz_dev - 1, greet_ring, 0)

    def greet_group(j, carry):
        m = (me_m + j // ny_dev) % nm
        y = (me_y + j % ny_dev) % ny_dev
        pl.semaphore_signal(barrier, inc=1, device_id=(me_z * ny_dev + y, m), device_id_type=MESH)
        return carry

    lax.fori_loop(1, group, greet_group, 0)

    fwd = {}
    fac = {}
    weight = {}
    for h in range(2):
        lanes = slice(h * BLOCK, (h + 1) * BLOCK)
        for d in range(3):
            fac[d, h] = jnp.broadcast_to(transmission[d : d + 1, lanes], (8, BLOCK))
            fwd[d, h] = jnp.broadcast_to(direction[d : d + 1, lanes], (8, BLOCK)) == 1
        total = jnp.sqrt(1.0 - transmission[0:1, lanes] * transmission[0:1, lanes])
        for d in range(1, 3):
            total = total * jnp.sqrt(1.0 - transmission[d : d + 1, lanes] * transmission[d : d + 1, lanes])
        weight[h] = total
    for h in range(2):
        coef_own[0, h * 4 : h * 4 + 4, :] = fac[2, h][:4]
        coef_own[1, h * 4 : h * 4 + 4, :] = jnp.where(fwd[2, h], 1.0, 0.0)[:4]

    eye = identity(chunk)

    loads[0].wait()
    for m in range(nm):
        for h in range(2):
            tile = nt(eye, prior_v[h * BLOCK : (h + 1) * BLOCK, m * chunk : (m + 1) * chunk])
            rows = [
                tile[y * nz + zh * ZLO : y * nz + (zh + 1) * ZLO] for zh in range(ny_dev) for y in range(YLO)
            ]
            turned[m, h] = jnp.concatenate(rows, axis=0).astype(BF16)

    def sweep_z(factor, forward):
        values = run([work[pl.ds(z, 8, stride=nz), :] for z in range(nz)], factor, forward)
        largest = jnp.abs(values[0])
        for z in range(nz):
            work[pl.ds(z, 8, stride=nz), :] = values[z]
            if z:
                largest = jnp.maximum(largest, jnp.abs(values[z]))
        largest = jnp.maximum(jnp.max(largest, axis=0, keepdims=True), 1e-30)
        return TOP / largest, largest * (1.0 / TOP)

    def two_rows(h, y, zh):
        start = h * chunk + y * nz + zh * ZLO
        return jnp.concatenate([work[start : start + ZLO, :], work[start + nz : start + nz + ZLO, :]], axis=0)

    loads[1].wait()
    pl.semaphore_wait(barrier, group - 1 + nz_dev - 1)

    sibling = me_x * 2 + 1 - me_core
    shared = pl.ds(PER_ROW + me_y, 1)
    direct = pl.ds(0, PER_ROW)
    for j in range(1, chips):
        to = (me_c, ((me_x + j) % chips) * 2 + me_core)
        part = blocks.at[me_m, shared]
        remote(part, part, gather_send.at[0], part_sem.at[j], to).start()
    pltpu.make_async_copy(turned.at[me_m], cur_a.at[:, me_m], s0_recv.at[0]).start()
    for j in range(1, nm):
        m = (me_m + j) % nm
        remote(turned.at[m], cur_a.at[:, me_m], s0_send.at[0], s0_recv.at[0], (me_c, m)).start()
    pltpu.make_async_copy(coef_own, coef.at[me_m], s0_recv.at[2]).start()
    for j in range(1, nm):
        m = (me_m + j) % nm
        remote(coef_own, coef.at[me_m], s0_send.at[2], s0_recv.at[2], (me_c, m)).start()
    for j in range(1, chips):
        to = (me_c, ((me_x + j) % chips) * 2 + me_core)
        part = blocks.at[me_m, direct]
        remote(part, part, gather_send.at[1], direct_sem.at[j], to).start()
    own = blocks.at[me_m]
    remote(own, own, gather_send.at[2], gather_recv.at[1], (me_c, sibling)).start()

    def over_y(m):
        part = blocks.at[m, shared]
        for i in range(1, ny_dev):
            to = (me_z * ny_dev + (me_y + i) % ny_dev, me_m)
            remote(part, part, gather_send.at[3], gather_recv.at[0], to).start()

    for j in range(1, chips):
        m = ((me_x + chips - j) % chips) * 2 + me_core
        await_bytes(blocks.at[m, shared], part_sem.at[j])
        over_y(m)

    loads[2].wait()

    def sweep_source(m, carry):
        for h in range(2):
            columns = pl.ds(pl.multiple_of(m * chunk, chunk), chunk)
            work[h * chunk : (h + 1) * chunk, :] = nt(eye, source_v[h * BLOCK : (h + 1) * BLOCK, columns])
        scale, unit = sweep_z(coef_own[0], coef_own[1] > 0.5)
        ss_send[m] = unit
        for zh in range(ny_dev):
            for h in range(2):
                for y in range(0, YLO, 2):
                    rows = pl.ds(m * YLO * ZLO + y * ZLO, 2 * ZLO)
                    s_send[zh, h, rows, :] = encode(two_rows(h, y, zh), scale)
        return carry

    lax.fori_loop(0, nm, sweep_source, 0)
    for i in range(1, ny_dev):
        y = (me_y + i) % ny_dev
        to = (me_z * ny_dev + y, me_m)
        remote(s_send.at[y], s_recv.at[me_y], s0_send.at[1], s0_recv.at[1], to).start()
        remote(ss_send, ss_recv.at[me_y], s0_send.at[3], s0_recv.at[3], to).start()
    pltpu.make_async_copy(s_send.at[me_y], s_recv.at[me_y], s0_recv.at[1]).start()
    pltpu.make_async_copy(ss_send, ss_recv.at[me_y], s0_recv.at[3]).start()
    for j in range(1, chips):
        part = blocks.at[((me_x + chips - j) % chips) * 2 + me_core, direct]
        await_bytes(part, direct_sem.at[j])
        remote(part, part, gather_send.at[4], gather_recv.at[1], (me_c, sibling)).start()
    if chips > 1:
        await_bytes(blocks.at[pl.ds(0, chips - 1), pl.ds(0, ny_dev - 1)], gather_recv.at[0])
    for j in range(1, chips):
        part = blocks.at[((me_x + chips - j) % chips) * 2 + me_core, pl.ds(PER_ROW, PER_ROW)]
        remote(part, part, gather_send.at[4], gather_recv.at[1], (me_c, sibling)).start()
    await_bytes(cur_a, s0_recv.at[0])
    await_bytes(coef, s0_recv.at[2])
    await_bytes(blocks.at[pl.ds(0, chips)], gather_recv.at[1])

    for iteration in range(ITERS):
        current = cur_a if iteration == 0 else cur_b
        last = iteration == ITERS - 1

        def scatter(j, carry):
            m = (me_m + 1 + j) % nm
            for h in range(2):
                row = m * 2 + h
                left = jnp.concatenate([current[pairs[row, k] % 2, pairs[row, k] // 2] for k in range(PER_ROW)], axis=1)
                right = jnp.concatenate([blocks[m, h * PER_ROW + k] for k in range(PER_ROW)], axis=1)
                total = nt(left, right)
                for zh in range(ny_dev):
                    for y in range(YLO):
                        work[h * chunk + y * nz + zh * ZLO : h * chunk + y * nz + (zh + 1) * ZLO, :] = total[
                            (zh * YLO + y) * ZLO : (zh * YLO + y + 1) * ZLO
                        ]
            scale, unit = sweep_z(coef[m, 0], coef[m, 1] > 0.5)
            xs_send[m] = unit
            for zh in range(ny_dev):
                for h in range(2):
                    for y in range(0, YLO, 2):
                        x_send[h, m * ny_dev + zh, y * ZLO : (y + 2) * ZLO, :] = encode(two_rows(h, y, zh), scale)
            send_codes(j, 0, True)
            return carry

        def send_codes(j, h, with_scale):
            m = (me_m + 1 + j) % nm
            slot = me_m * ny_dev + me_y
            for i in range(ny_dev):
                y = (me_y + 1 + i) % ny_dev
                to = (me_z * ny_dev + y, m)

                def send():
                    src, dst = x_send.at[h, m * ny_dev + y], x_recv.at[h, slot]
                    remote(src, dst, x_sem.at[h], x_sem.at[2 + h], to).start()
                    if with_scale:
                        remote(xs_send.at[m], xs_recv.at[slot], scale_sem.at[0], scale_sem.at[1], to).start()

                def keep():
                    src, dst = x_send.at[h, m * ny_dev + y], x_recv.at[h, slot]
                    pltpu.make_async_copy(src, dst, x_sem.at[2 + h]).start()
                    if with_scale:
                        pltpu.make_async_copy(xs_send.at[m], xs_recv.at[slot], scale_sem.at[1]).start()

                if i < ny_dev - 1:
                    send()
                else:
                    pl.when(j < nm - 1)(send)
                    pl.when(j == nm - 1)(keep)

        def send_second(j, carry):
            send_codes(j, 1, False)
            return carry

        lax.fori_loop(0, nm, scatter, 0)
        lax.fori_loop(0, nm, send_second, 0)

        def send_ring(h, scale, codes, into, sem, unit, units, unit_sem):
            def one(j, carry):
                z = (me_z + 1 + j) % nz_dev
                codes[h, z] = encode(ends[h, pl.ds(z * per_z, per_z), :], scale)
                to = (z * ny_dev + me_y, me_m)

                @pl.when(j < nz_dev - 1)
                def _():
                    remote(codes.at[h, z], into.at[h, me_z], sem.at[h], sem.at[2 + h], to).start()
                    remote(
                        unit.at[h], units.at[h, me_z], scale_sem.at[unit_sem + h], scale_sem.at[unit_sem + 2 + h], to
                    ).start()

                @pl.when(j == nz_dev - 1)
                def _():
                    pltpu.make_async_copy(codes.at[h, z], into.at[h, me_z], sem.at[2 + h]).start()
                    pltpu.make_async_copy(unit.at[h], units.at[h, me_z], scale_sem.at[unit_sem + 2 + h]).start()

                return carry

            lax.fori_loop(0, nz_dev, one, 0)

        def wide_fac(h):
            return jnp.concatenate([fac[0, h]] * YLO, axis=0)

        def wide_fwd(h):
            tile = jnp.broadcast_to(direction[0:1, h * BLOCK : (h + 1) * BLOCK], (8, BLOCK))
            return jnp.concatenate([tile] * YLO, axis=0) == 1

        def hand_on(h):
            def unpack(m, carry):
                rows = pl.ds(m * YLO * ZLO, YLO * ZLO)
                got = []
                for x in range(XLO):
                    value = decode(x_recv[h, m * ny_dev + x]) * (xs_recv[m * ny_dev + x] * weight[h])
                    value += decode(s_recv[x, h, rows, :]) * (ss_recv[x, m] * weight[h])
                    planes[h, x, rows, :] = value
                    got.append(value)
                t, f = wide_fac(h), wide_fwd(h)
                end = jnp.where(f, got[0], got[XLO - 1])
                for x in range(1, XLO):
                    end = end * t + jnp.where(f, got[x], got[XLO - 1 - x])
                ends[h, rows, :] = end
                return carry

            lax.fori_loop(0, nm, unpack, 0)
            values = [ends[h, y * ZLO : (y + 1) * ZLO, :] for y in range(ny)]
            values = run(values, fac[1, h], fwd[1, h])
            largest = jnp.full((8, BLOCK), 1e-30, F32)
            for y in range(ny):
                ends[h, y * ZLO : (y + 1) * ZLO, :] = values[y]
                largest = jnp.maximum(largest, jnp.abs(values[y]))
            largest = jnp.max(largest, axis=0, keepdims=True)
            es_send[h] = largest * (1.0 / TOP)
            send_ring(h, TOP / largest, e_send, e_recv, e_sem, es_send, es_recv, 2)

        def sweep_y(h):
            def one(x, carry):
                values = [planes[h, x, y * ZLO : (y + 1) * ZLO, :] for y in range(ny)]
                values = run(values, fac[1, h], fwd[1, h])
                for y in range(ny):
                    planes[h, x, y * ZLO : (y + 1) * ZLO, :] = values[y]
                return carry

            lax.fori_loop(0, XLO, one, 0)

        def scan_ring(h):
            largest = jnp.full((8, BLOCK), 1e-30, F32)
            leap = fac[0, h] * fac[0, h]
            leap = leap * leap
            f = fwd[0, h]
            for part in range(per_z // 16):
                got = [
                    decode(e_recv[h, z, part * 16 : part * 16 + 16, :]) * es_recv[h, z] for z in range(nz_dev)
                ]
                for i in range(2):
                    given = [g[i * 8 : i * 8 + 8] for g in got]
                    ordered = [jnp.where(f, given[s], given[nz_dev - 1 - s]) for s in range(nz_dev)]
                    taken = [jnp.zeros_like(ordered[0])]
                    for s in range(nz_dev - 1):
                        taken.append(leap * taken[-1] + ordered[s])
                    for z in range(nz_dev):
                        value = jnp.where(f, taken[z], taken[nz_dev - 1 - z])
                        start = z * per_z + part * 16 + i * 8
                        ends[h, start : start + 8, :] = value
                        largest = jnp.maximum(largest, jnp.abs(value))
            largest = jnp.max(largest, axis=0, keepdims=True)
            bs_send[h] = largest * (1.0 / TOP)
            send_ring(h, TOP / largest, b_send, b_recv, b_sem, bs_send, bs_recv, 6)

        def finish_half(h):
            def inflow(z, carry):
                ends[h, pl.ds(z * per_z, per_z), :] = decode(b_recv[h, z]) * bs_recv[h, z]
                return carry

            lax.fori_loop(0, nz_dev, inflow, 0)

            def finish(j, carry):
                m = (me_m + 1 + j) % nm
                rows = pl.ds(m * YLO * ZLO, YLO * ZLO)
                t, f = wide_fac(h), wide_fwd(h)
                given = [planes[h, x, rows, :] for x in range(XLO)]
                value = ends[h, rows, :]
                swept = []
                for x in range(XLO):
                    value = t * value + jnp.where(f, given[x], given[XLO - 1 - x])
                    swept.append(value)
                for x in range(XLO):
                    result = jnp.where(f, swept[x], swept[XLO - 1 - x]).astype(BF16)
                    if last:
                        f_send[h, x, rows, :] = result
                    else:
                        c_send[h, m * ny_dev + x] = result
                if not last:
                    for i in range(ny_dev):
                        y = (me_y + 1 + i) % ny_dev
                        to = (me_z * ny_dev + y, m)
                        into = cur_b.at[h, me_m, pl.ds(me_y * YLO * ZLO, YLO * ZLO), :]

                        def send():
                            remote(c_send.at[h, m * ny_dev + y], into, c_sem.at[h], c_sem.at[2 + h], to).start()

                        def keep():
                            pltpu.make_async_copy(c_send.at[h, m * ny_dev + y], into, c_sem.at[2 + h]).start()

                        if i < ny_dev - 1:
                            send()
                        else:
                            pl.when(j < nm - 1)(send)
                            pl.when(j == nm - 1)(keep)
                return carry

            lax.fori_loop(0, nm, finish, 0)
            if last:
                for i in range(1, ny_dev):
                    y = (me_y + i) % ny_dev
                    to = (me_z * ny_dev + y, me_m)
                    remote(f_send.at[h, y], f_recv.at[h, me_y], f_sem.at[h], f_sem.at[2 + h], to).start()
                pltpu.make_async_copy(f_send.at[h, me_y], f_recv.at[h, me_y], f_sem.at[2 + h]).start()

        await_bytes(x_recv.at[0], x_sem.at[2])
        await_bytes(xs_recv, scale_sem.at[1])
        if iteration == 0:
            await_bytes(s_recv, s0_recv.at[1])
            await_bytes(ss_recv, s0_recv.at[3])
        hand_on(0)
        await_bytes(x_recv.at[1], x_sem.at[3])
        hand_on(1)
        sweep_y(0)
        for h in range(2):
            await_bytes(e_recv.at[h], e_sem.at[2 + h])
            await_bytes(es_recv.at[h], scale_sem.at[4 + h])
            scan_ring(h)
            if h == 0:
                sweep_y(1)
        for h in range(2):
            await_bytes(b_recv.at[h], b_sem.at[2 + h])
            await_bytes(bs_recv.at[h], scale_sem.at[8 + h])
            finish_half(h)
        await_bytes(xs_recv.at[pl.ds(0, group - 1)], scale_sem.at[0])
        for h in range(2):
            await_bytes(x_send.at[h, pl.ds(0, group - 1)], x_sem.at[h])
            await_bytes(e_send.at[h, pl.ds(0, nz_dev - 1)], e_sem.at[h])
            await_bytes(es_recv.at[h, pl.ds(0, nz_dev - 1)], scale_sem.at[2 + h])
            await_bytes(b_send.at[h, pl.ds(0, nz_dev - 1)], b_sem.at[h])
            await_bytes(bs_recv.at[h, pl.ds(0, nz_dev - 1)], scale_sem.at[6 + h])
        if not last:
            for h in range(2):
                await_bytes(cur_b.at[h], c_sem.at[2 + h])
                await_bytes(c_send.at[h, pl.ds(0, group - 1)], c_sem.at[h])

    await_bytes(turned.at[pl.ds(0, nm - 1)], s0_send.at[0])
    await_bytes(s_send.at[pl.ds(0, ny_dev - 1)], s0_send.at[1])
    await_bytes(ss_recv.at[pl.ds(0, ny_dev - 1)], s0_send.at[3])
    await_bytes(coef.at[pl.ds(0, nm - 1)], s0_send.at[2])
    if chips > 1:
        await_bytes(blocks.at[0, pl.ds(0, chips - 1)], gather_send.at[0])
        await_bytes(blocks.at[pl.ds(0, chips - 1), direct], gather_send.at[1])
        await_bytes(blocks.at[pl.ds(0, chips - 1), pl.ds(0, ny_dev - 1)], gather_send.at[3])
        await_bytes(blocks.at[pl.ds(0, chips - 1)], gather_send.at[4])
    await_bytes(blocks.at[0], gather_send.at[2])
    wide = identity(BLOCK)
    for h in range(2):
        await_bytes(f_recv.at[h], f_sem.at[2 + h])
        for m in range(nm):
            parts = [f_recv[h, zh, m * YLO * ZLO : (m + 1) * YLO * ZLO, :].astype(F32) for zh in range(ny_dev)]
            rows = [parts[zh][y * ZLO : (y + 1) * ZLO] for y in range(YLO) for zh in range(ny_dev)]
            tile = jnp.concatenate(rows, axis=0).astype(BF16)
            out[h * BLOCK : (h + 1) * BLOCK, m * chunk : (m + 1) * chunk] = nt(wide, tile).astype(BF16)
    for h in range(2):
        await_bytes(f_send.at[h, pl.ds(0, ny_dev - 1)], f_sem.at[h])


def local(dims, source, prior, coupling, pairs, transmission, direction):
    nm, ny_dev, nz_dev, ny, nz = dims
    modes = source.shape[0]
    group = nm * ny_dev
    chunk = YLO * nz
    tall = ny * ZLO
    per_z = tall // nz_dev
    vmem = pl.BlockSpec(memory_space=pltpu.VMEM)
    hbm = pl.BlockSpec(memory_space=pltpu.HBM)
    dma = pltpu.SemaphoreType.DMA
    result = pl.pallas_call(
        functools.partial(kernel, dims),
        out_shape=jax.ShapeDtypeStruct((modes, ny * nz), BF16),
        in_specs=[hbm, hbm, hbm, pl.BlockSpec(memory_space=pltpu.SMEM), vmem, vmem],
        out_specs=vmem,
        scratch_shapes=[
            pltpu.VMEM((modes, ny * nz), BF16),
            pltpu.VMEM((modes, ny * nz), BF16),
            pltpu.VMEM((2, nm, chunk, BLOCK), BF16),
            pltpu.VMEM((2, nm, chunk, BLOCK), BF16),
            pltpu.VMEM((nm, 2, chunk, BLOCK), BF16),
            pltpu.VMEM((ny_dev, 2, tall, BLOCK), I16),
            pltpu.VMEM((ny_dev, 2, tall, BLOCK), I16),
            pltpu.VMEM((nm, 1, BLOCK), F32),
            pltpu.VMEM((ny_dev, nm, 1, BLOCK), F32),
            pltpu.VMEM((nm, 2 * PER_ROW, BLOCK, BLOCK), BF16),
            pltpu.VMEM((2, 8, BLOCK), F32),
            pltpu.VMEM((nm, 2, 8, BLOCK), F32),
            pltpu.VMEM((2 * chunk, BLOCK), F32),
            pltpu.VMEM((2, group, YLO * ZLO, BLOCK), I16),
            pltpu.VMEM((2, group, YLO * ZLO, BLOCK), I16),
            pltpu.VMEM((nm, 1, BLOCK), F32),
            pltpu.VMEM((group, 1, BLOCK), F32),
            pltpu.VMEM((2, XLO, tall, BLOCK), F32),
            pltpu.VMEM((2, tall, BLOCK), F32),
            pltpu.VMEM((2, nz_dev, per_z, BLOCK), I16),
            pltpu.VMEM((2, nz_dev, per_z, BLOCK), I16),
            pltpu.VMEM((2, 1, BLOCK), F32),
            pltpu.VMEM((2, nz_dev, 1, BLOCK), F32),
            pltpu.VMEM((2, nz_dev, per_z, BLOCK), I16),
            pltpu.VMEM((2, nz_dev, per_z, BLOCK), I16),
            pltpu.VMEM((2, 1, BLOCK), F32),
            pltpu.VMEM((2, nz_dev, 1, BLOCK), F32),
            pltpu.VMEM((2, group, YLO * ZLO, BLOCK), BF16),
            pltpu.VMEM((2, ny_dev, tall, BLOCK), BF16),
            pltpu.VMEM((2, ny_dev, tall, BLOCK), BF16),
            dma((3,)),
            dma((4,)),
            dma((4,)),
            dma((5,)),
            dma((2,)),
            dma((nm // 2,)),
            dma((nm // 2,)),
            dma((4,)),
            dma((4,)),
            dma((4,)),
            dma((4,)),
            dma((4,)),
            dma((10,)),
        ],
        compiler_params=pltpu.CompilerParams(
            collective_id=0, has_side_effects=True, vmem_limit_bytes=40 * 1024 * 1024
        ),
        cost_estimate=pl.CostEstimate(flops=600_000_000, bytes_accessed=2_000_000, transcendentals=0),
    )(
        source.reshape(modes, ny * nz),
        prior.reshape(modes, ny * nz),
        coupling.reshape(2 * PER_ROW, BLOCK, BLOCK),
        pairs,
        transmission,
        direction,
    )
    return result.reshape(modes, 1, ny * nz)


def build(mesh, ny, nz):
    nm = mesh.shape["mode"]
    ny_dev = nz // ZLO
    nz_dev = mesh.shape["cell"] // ny_dev
    in_specs = (
        P("mode", "cell", None),
        P("mode", "cell", None),
        P("mode", None, None, None),
        P(),
        P(None, "mode"),
        P(None, "mode"),
    )
    body = functools.partial(local, (nm, ny_dev, nz_dev, ny, nz))
    return jax.shard_map(body, mesh=mesh, in_specs=in_specs, out_specs=P("mode", "cell", None), check_vma=False)


def solution(mesh):
    return build(mesh, 32, 32)
```

```python
import functools

import jax
import jax.numpy as jnp
from jax import lax
from jax.experimental import pallas as pl
from jax.experimental.pallas import tpu as pltpu
from jax.sharding import PartitionSpec as P

ITERS = 2
BLOCK = 128
PER_ROW = 4
ZLO = 8
YLO = 4
XLO = 4
TOP = 32767.0
F32 = jnp.float32
BF16 = jnp.bfloat16
I16 = jnp.int16
MESH = pl.DeviceIdType.MESH


def nt(left, right):
    return lax.dot_general(left, right, (((1,), (1,)), ((), ())), preferred_element_type=F32)


def identity(size):
    rows = lax.broadcasted_iota(jnp.int32, (size, size), 0)
    columns = lax.broadcasted_iota(jnp.int32, (size, size), 1)
    return jnp.where(rows == columns, 1.0, 0.0).astype(BF16)


def run(values, factor, forward):
    n = len(values)
    ordered = [jnp.where(forward, values[s], values[n - 1 - s]) for s in range(n)]
    swept = [ordered[0]]
    for s in range(1, n):
        swept.append(factor * swept[-1] + ordered[s])
    return [jnp.where(forward, swept[s], swept[n - 1 - s]) for s in range(n)]


def encode(values, scale):
    return jnp.round(values * scale).astype(jnp.int32).astype(I16)


def decode(codes):
    return codes.astype(jnp.int32).astype(F32)


def kernel(
    dims,
    source,
    prior,
    coupling,
    pairs_in,
    transmission_in,
    direction_in,
    out,
    pairs,
    transmission,
    direction,
    source_v,
    prior_v,
    cur_a,
    cur_b,
    turned,
    s_send,
    s_recv,
    ss_send,
    ss_recv,
    blocks,
    coef_own,
    coef,
    work,
    x_send,
    x_recv,
    xs_send,
    xs_recv,
    planes,
    ends,
    e_send,
    e_recv,
    es_send,
    es_recv,
    b_send,
    b_recv,
    bs_send,
    bs_recv,
    c_send,
    f_send,
    f_recv,
    round_sem,
    in_sem,
    s0_send,
    s0_recv,
    gather_send,
    gather_recv,
    direct_sem,
    part_sem,
    x_sem,
    e_sem,
    b_sem,
    c_sem,
    f_sem,
    scale_sem,
):
    nm, ny_dev, nz_dev, ny, nz = dims
    chips = nm // 2
    chunk = YLO * nz
    tall = ny * ZLO
    per_z = tall // nz_dev
    me_m = lax.axis_index("mode")
    me_c = lax.axis_index("cell")
    me_z, me_y = me_c // ny_dev, me_c % ny_dev
    me_x, me_core = me_m // 2, me_m % 2

    def remote(src, dst, send, recv, to):
        return pltpu.make_async_remote_copy(
            src_ref=src, dst_ref=dst, send_sem=send, recv_sem=recv, device_id=to, device_id_type=MESH
        )

    def await_bytes(ref, sem):
        pltpu.make_async_copy(ref, ref, sem).wait()

    loads = [
        pltpu.make_async_copy(prior, prior_v, in_sem.at[0]),
        pltpu.make_async_copy(coupling, blocks.at[me_m], in_sem.at[1]),
        pltpu.make_async_copy(source, source_v, in_sem.at[2]),
    ]
    small = [
        pltpu.make_async_copy(transmission_in, transmission, in_sem.at[3]),
        pltpu.make_async_copy(direction_in, direction, in_sem.at[4]),
        pltpu.make_async_copy(pairs_in, pairs, in_sem.at[5]),
    ]

    barrier = pltpu.get_barrier_semaphore()
    group = nm * ny_dev
    near = [(me_z * ny_dev + (me_y + i) % ny_dev, me_m) for i in range(1, ny_dev)]
    near += [(me_c, (me_m + j) % nm) for j in range(1, nm)]

    def ring(step):
        return [((me_z + z) % nz_dev * ny_dev + me_y, me_m) for z in sorted({step % nz_dev, -step % nz_dev} - {0})]

    near += ring(1)
    for to in near:
        pl.semaphore_signal(barrier, inc=1, device_id=to, device_id_type=MESH)
    for load in small + loads:
        load.start()

    rounds = []
    while 2 ** len(rounds) < nz_dev // 2:
        rounds.append(2 ** len(rounds))

    def meet(r):
        if r and r - 1 < len(rounds):
            pl.semaphore_wait(round_sem.at[r - 1], 2)
        if r < len(rounds):
            for to in ring(rounds[r]):
                pl.semaphore_signal(round_sem.at[r], inc=1, device_id=to, device_id_type=MESH)

    for load in small:
        load.wait()
    fwd = {}
    fac = {}
    weight = {}
    for h in range(2):
        lanes = slice(h * BLOCK, (h + 1) * BLOCK)
        for d in range(3):
            fac[d, h] = jnp.broadcast_to(transmission[d : d + 1, lanes], (8, BLOCK))
            fwd[d, h] = jnp.broadcast_to(direction[d : d + 1, lanes], (8, BLOCK)) == 1
        total = jnp.sqrt(1.0 - transmission[0:1, lanes] * transmission[0:1, lanes])
        for d in range(1, 3):
            total = total * jnp.sqrt(1.0 - transmission[d : d + 1, lanes] * transmission[d : d + 1, lanes])
        weight[h] = total
    for h in range(2):
        coef_own[0, h * 4 : h * 4 + 4, :] = fac[2, h][:4]
        coef_own[1, h * 4 : h * 4 + 4, :] = jnp.where(fwd[2, h], 1.0, 0.0)[:4]

    eye = identity(chunk)

    loads[0].wait()
    for m in range(nm):
        for h in range(2):
            tile = nt(eye, prior_v[h * BLOCK : (h + 1) * BLOCK, m * chunk : (m + 1) * chunk])
            rows = [
                tile[y * nz + zh * ZLO : y * nz + (zh + 1) * ZLO] for zh in range(ny_dev) for y in range(YLO)
            ]
            turned[m, h] = jnp.concatenate(rows, axis=0).astype(BF16)

    def sweep_z(factor, forward):
        values = run([work[pl.ds(z, 8, stride=nz), :] for z in range(nz)], factor, forward)
        largest = jnp.abs(values[0])
        for z in range(nz):
            work[pl.ds(z, 8, stride=nz), :] = values[z]
            if z:
                largest = jnp.maximum(largest, jnp.abs(values[z]))
        largest = jnp.maximum(jnp.max(largest, axis=0, keepdims=True), 1e-30)
        return TOP / largest, largest * (1.0 / TOP)

    def two_rows(h, y, zh):
        start = h * chunk + y * nz + zh * ZLO
        return jnp.concatenate([work[start : start + ZLO, :], work[start + nz : start + nz + ZLO, :]], axis=0)

    loads[1].wait()
    pl.semaphore_wait(barrier, len(near))
    meet(0)

    sibling = me_x * 2 + 1 - me_core
    shared = pl.ds(PER_ROW + me_y, 1)
    direct = pl.ds(0, PER_ROW)
    for j in range(1, chips):
        to = (me_c, ((me_x + j) % chips) * 2 + me_core)
        part = blocks.at[me_m, shared]
        remote(part, part, gather_send.at[0], part_sem.at[j], to).start()
    pltpu.make_async_copy(turned.at[me_m], cur_a.at[:, me_m], s0_recv.at[0]).start()
    for j in range(1, nm):
        m = (me_m + j) % nm
        remote(turned.at[m], cur_a.at[:, me_m], s0_send.at[0], s0_recv.at[0], (me_c, m)).start()
    pltpu.make_async_copy(coef_own, coef.at[me_m], s0_recv.at[2]).start()
    for j in range(1, nm):
        m = (me_m + j) % nm
        remote(coef_own, coef.at[me_m], s0_send.at[2], s0_recv.at[2], (me_c, m)).start()
    for j in range(1, chips):
        to = (me_c, ((me_x + j) % chips) * 2 + me_core)
        part = blocks.at[me_m, direct]
        remote(part, part, gather_send.at[1], direct_sem.at[j], to).start()
    own = blocks.at[me_m]
    remote(own, own, gather_send.at[2], gather_recv.at[1], (me_c, sibling)).start()

    def over_y(m):
        part = blocks.at[m, shared]
        for i in range(1, ny_dev):
            to = (me_z * ny_dev + (me_y + i) % ny_dev, me_m)
            remote(part, part, gather_send.at[3], gather_recv.at[0], to).start()

    meet(1)
    for j in range(1, chips):
        m = ((me_x + chips - j) % chips) * 2 + me_core
        await_bytes(blocks.at[m, shared], part_sem.at[j])
        over_y(m)

    meet(2)
    loads[2].wait()

    def sweep_source(m, carry):
        for h in range(2):
            columns = pl.ds(pl.multiple_of(m * chunk, chunk), chunk)
            work[h * chunk : (h + 1) * chunk, :] = nt(eye, source_v[h * BLOCK : (h + 1) * BLOCK, columns])
        scale, unit = sweep_z(coef_own[0], coef_own[1] > 0.5)
        ss_send[m] = unit
        for zh in range(ny_dev):
            for h in range(2):
                for y in range(0, YLO, 2):
                    rows = pl.ds(m * YLO * ZLO + y * ZLO, 2 * ZLO)
                    s_send[zh, h, rows, :] = encode(two_rows(h, y, zh), scale)
        return carry

    lax.fori_loop(0, nm, sweep_source, 0)
    for i in range(1, ny_dev):
        y = (me_y + i) % ny_dev
        to = (me_z * ny_dev + y, me_m)
        remote(s_send.at[y], s_recv.at[me_y], s0_send.at[1], s0_recv.at[1], to).start()
        remote(ss_send, ss_recv.at[me_y], s0_send.at[3], s0_recv.at[3], to).start()
    pltpu.make_async_copy(s_send.at[me_y], s_recv.at[me_y], s0_recv.at[1]).start()
    pltpu.make_async_copy(ss_send, ss_recv.at[me_y], s0_recv.at[3]).start()
    for j in range(1, chips):
        part = blocks.at[((me_x + chips - j) % chips) * 2 + me_core, direct]
        await_bytes(part, direct_sem.at[j])
        remote(part, part, gather_send.at[4], gather_recv.at[1], (me_c, sibling)).start()
    if chips > 1:
        await_bytes(blocks.at[pl.ds(0, chips - 1), pl.ds(0, ny_dev - 1)], gather_recv.at[0])
    for j in range(1, chips):
        part = blocks.at[((me_x + chips - j) % chips) * 2 + me_core, pl.ds(PER_ROW, PER_ROW)]
        remote(part, part, gather_send.at[4], gather_recv.at[1], (me_c, sibling)).start()
    meet(3)
    await_bytes(cur_a, s0_recv.at[0])
    await_bytes(coef, s0_recv.at[2])
    await_bytes(blocks.at[pl.ds(0, chips)], gather_recv.at[1])

    for iteration in range(ITERS):
        current = cur_a if iteration == 0 else cur_b
        last = iteration == ITERS - 1

        def scatter(j, carry):
            m = (me_m + 1 + j) % nm
            for h in range(2):
                row = m * 2 + h
                left = jnp.concatenate([current[pairs[k, row] % 2, pairs[k, row] // 2] for k in range(PER_ROW)], axis=1)
                right = jnp.concatenate([blocks[m, h * PER_ROW + k] for k in range(PER_ROW)], axis=1)
                total = nt(left, right)
                for zh in range(ny_dev):
                    for y in range(YLO):
                        work[h * chunk + y * nz + zh * ZLO : h * chunk + y * nz + (zh + 1) * ZLO, :] = total[
                            (zh * YLO + y) * ZLO : (zh * YLO + y + 1) * ZLO
                        ]
            scale, unit = sweep_z(coef[m, 0], coef[m, 1] > 0.5)
            xs_send[m] = unit
            for zh in range(ny_dev):
                for h in range(2):
                    for y in range(0, YLO, 2):
                        x_send[h, m * ny_dev + zh, y * ZLO : (y + 2) * ZLO, :] = encode(two_rows(h, y, zh), scale)
            send_codes(j, 0, True)
            return carry

        def send_codes(j, h, with_scale):
            m = (me_m + 1 + j) % nm
            slot = me_m * ny_dev + me_y
            for i in range(ny_dev):
                y = (me_y + 1 + i) % ny_dev
                to = (me_z * ny_dev + y, m)

                def send():
                    src, dst = x_send.at[h, m * ny_dev + y], x_recv.at[h, slot]
                    remote(src, dst, x_sem.at[h], x_sem.at[2 + h], to).start()
                    if with_scale:
                        remote(xs_send.at[m], xs_recv.at[slot], scale_sem.at[0], scale_sem.at[1], to).start()

                def keep():
                    src, dst = x_send.at[h, m * ny_dev + y], x_recv.at[h, slot]
                    pltpu.make_async_copy(src, dst, x_sem.at[2 + h]).start()
                    if with_scale:
                        pltpu.make_async_copy(xs_send.at[m], xs_recv.at[slot], scale_sem.at[1]).start()

                if i < ny_dev - 1:
                    send()
                else:
                    pl.when(j < nm - 1)(send)
                    pl.when(j == nm - 1)(keep)

        def send_second(j, carry):
            send_codes(j, 1, False)
            return carry

        lax.fori_loop(0, nm, scatter, 0)
        lax.fori_loop(0, nm, send_second, 0)

        def send_ring(h, scale, codes, into, sem, unit, units, unit_sem):
            def one(j, carry):
                z = (me_z + 1 + j) % nz_dev
                codes[h, z] = encode(ends[h, pl.ds(z * per_z, per_z), :], scale)
                to = (z * ny_dev + me_y, me_m)

                @pl.when(j < nz_dev - 1)
                def _():
                    remote(codes.at[h, z], into.at[h, me_z], sem.at[h], sem.at[2 + h], to).start()
                    remote(
                        unit.at[h], units.at[h, me_z], scale_sem.at[unit_sem + h], scale_sem.at[unit_sem + 2 + h], to
                    ).start()

                @pl.when(j == nz_dev - 1)
                def _():
                    pltpu.make_async_copy(codes.at[h, z], into.at[h, me_z], sem.at[2 + h]).start()
                    pltpu.make_async_copy(unit.at[h], units.at[h, me_z], scale_sem.at[unit_sem + 2 + h]).start()

                return carry

            lax.fori_loop(0, nz_dev, one, 0)

        def wide_fac(h):
            return jnp.concatenate([fac[0, h]] * YLO, axis=0)

        def wide_fwd(h):
            tile = jnp.broadcast_to(direction[0:1, h * BLOCK : (h + 1) * BLOCK], (8, BLOCK))
            return jnp.concatenate([tile] * YLO, axis=0) == 1

        def hand_on(h):
            def unpack(m, carry):
                rows = pl.ds(m * YLO * ZLO, YLO * ZLO)
                got = []
                for x in range(XLO):
                    value = decode(x_recv[h, m * ny_dev + x]) * (xs_recv[m * ny_dev + x] * weight[h])
                    value += decode(s_recv[x, h, rows, :]) * (ss_recv[x, m] * weight[h])
                    planes[h, x, rows, :] = value
                    got.append(value)
                t, f = wide_fac(h), wide_fwd(h)
                end = jnp.where(f, got[0], got[XLO - 1])
                for x in range(1, XLO):
                    end = end * t + jnp.where(f, got[x], got[XLO - 1 - x])
                ends[h, rows, :] = end
                return carry

            lax.fori_loop(0, nm, unpack, 0)
            values = [ends[h, y * ZLO : (y + 1) * ZLO, :] for y in range(ny)]
            values = run(values, fac[1, h], fwd[1, h])
            largest = jnp.full((8, BLOCK), 1e-30, F32)
            for y in range(ny):
                ends[h, y * ZLO : (y + 1) * ZLO, :] = values[y]
                largest = jnp.maximum(largest, jnp.abs(values[y]))
            largest = jnp.max(largest, axis=0, keepdims=True)
            es_send[h] = largest * (1.0 / TOP)
            send_ring(h, TOP / largest, e_send, e_recv, e_sem, es_send, es_recv, 2)

        def sweep_y(h):
            def one(x, carry):
                values = [planes[h, x, y * ZLO : (y + 1) * ZLO, :] for y in range(ny)]
                values = run(values, fac[1, h], fwd[1, h])
                for y in range(ny):
                    planes[h, x, y * ZLO : (y + 1) * ZLO, :] = values[y]
                return carry

            lax.fori_loop(0, XLO, one, 0)

        def scan_ring(h):
            largest = jnp.full((8, BLOCK), 1e-30, F32)
            leap = fac[0, h] * fac[0, h]
            leap = leap * leap
            f = fwd[0, h]
            for part in range(per_z // 16):
                got = [
                    decode(e_recv[h, z, part * 16 : part * 16 + 16, :]) * es_recv[h, z] for z in range(nz_dev)
                ]
                for i in range(2):
                    given = [g[i * 8 : i * 8 + 8] for g in got]
                    ordered = [jnp.where(f, given[s], given[nz_dev - 1 - s]) for s in range(nz_dev)]
                    taken = [jnp.zeros_like(ordered[0])]
                    for s in range(nz_dev - 1):
                        taken.append(leap * taken[-1] + ordered[s])
                    for z in range(nz_dev):
                        value = jnp.where(f, taken[z], taken[nz_dev - 1 - z])
                        start = z * per_z + part * 16 + i * 8
                        ends[h, start : start + 8, :] = value
                        largest = jnp.maximum(largest, jnp.abs(value))
            largest = jnp.max(largest, axis=0, keepdims=True)
            bs_send[h] = largest * (1.0 / TOP)
            send_ring(h, TOP / largest, b_send, b_recv, b_sem, bs_send, bs_recv, 6)

        def finish_half(h):
            def inflow(z, carry):
                ends[h, pl.ds(z * per_z, per_z), :] = decode(b_recv[h, z]) * bs_recv[h, z]
                return carry

            lax.fori_loop(0, nz_dev, inflow, 0)

            def finish(j, carry):
                m = (me_m + 1 + j) % nm
                rows = pl.ds(m * YLO * ZLO, YLO * ZLO)
                t, f = wide_fac(h), wide_fwd(h)
                given = [planes[h, x, rows, :] for x in range(XLO)]
                value = ends[h, rows, :]
                swept = []
                for x in range(XLO):
                    value = t * value + jnp.where(f, given[x], given[XLO - 1 - x])
                    swept.append(value)
                for x in range(XLO):
                    result = jnp.where(f, swept[x], swept[XLO - 1 - x]).astype(BF16)
                    if last:
                        f_send[h, x, rows, :] = result
                    else:
                        c_send[h, m * ny_dev + x] = result
                if not last:
                    for i in range(ny_dev):
                        y = (me_y + 1 + i) % ny_dev
                        to = (me_z * ny_dev + y, m)
                        into = cur_b.at[h, me_m, pl.ds(me_y * YLO * ZLO, YLO * ZLO), :]

                        def send():
                            remote(c_send.at[h, m * ny_dev + y], into, c_sem.at[h], c_sem.at[2 + h], to).start()

                        def keep():
                            pltpu.make_async_copy(c_send.at[h, m * ny_dev + y], into, c_sem.at[2 + h]).start()

                        if i < ny_dev - 1:
                            send()
                        else:
                            pl.when(j < nm - 1)(send)
                            pl.when(j == nm - 1)(keep)
                return carry

            lax.fori_loop(0, nm, finish, 0)
            if last:
                for i in range(1, ny_dev):
                    y = (me_y + i) % ny_dev
                    to = (me_z * ny_dev + y, me_m)
                    remote(f_send.at[h, y], f_recv.at[h, me_y], f_sem.at[h], f_sem.at[2 + h], to).start()
                pltpu.make_async_copy(f_send.at[h, me_y], f_recv.at[h, me_y], f_sem.at[2 + h]).start()

        await_bytes(x_recv.at[0], x_sem.at[2])
        await_bytes(xs_recv, scale_sem.at[1])
        if iteration == 0:
            await_bytes(s_recv, s0_recv.at[1])
            await_bytes(ss_recv, s0_recv.at[3])
        hand_on(0)
        await_bytes(x_recv.at[1], x_sem.at[3])
        hand_on(1)
        sweep_y(0)
        for h in range(2):
            await_bytes(e_recv.at[h], e_sem.at[2 + h])
            await_bytes(es_recv.at[h], scale_sem.at[4 + h])
            scan_ring(h)
            if h == 0:
                sweep_y(1)
        for h in range(2):
            await_bytes(b_recv.at[h], b_sem.at[2 + h])
            await_bytes(bs_recv.at[h], scale_sem.at[8 + h])
            finish_half(h)
        await_bytes(xs_recv.at[pl.ds(0, group - 1)], scale_sem.at[0])
        for h in range(2):
            await_bytes(x_send.at[h, pl.ds(0, group - 1)], x_sem.at[h])
            await_bytes(e_send.at[h, pl.ds(0, nz_dev - 1)], e_sem.at[h])
            await_bytes(es_recv.at[h, pl.ds(0, nz_dev - 1)], scale_sem.at[2 + h])
            await_bytes(b_send.at[h, pl.ds(0, nz_dev - 1)], b_sem.at[h])
            await_bytes(bs_recv.at[h, pl.ds(0, nz_dev - 1)], scale_sem.at[6 + h])
        if not last:
            for h in range(2):
                await_bytes(cur_b.at[h], c_sem.at[2 + h])
                await_bytes(c_send.at[h, pl.ds(0, group - 1)], c_sem.at[h])

    await_bytes(turned.at[pl.ds(0, nm - 1)], s0_send.at[0])
    await_bytes(s_send.at[pl.ds(0, ny_dev - 1)], s0_send.at[1])
    await_bytes(ss_recv.at[pl.ds(0, ny_dev - 1)], s0_send.at[3])
    await_bytes(coef.at[pl.ds(0, nm - 1)], s0_send.at[2])
    if chips > 1:
        await_bytes(blocks.at[0, pl.ds(0, chips - 1)], gather_send.at[0])
        await_bytes(blocks.at[pl.ds(0, chips - 1), direct], gather_send.at[1])
        await_bytes(blocks.at[pl.ds(0, chips - 1), pl.ds(0, ny_dev - 1)], gather_send.at[3])
        await_bytes(blocks.at[pl.ds(0, chips - 1)], gather_send.at[4])
    await_bytes(blocks.at[0], gather_send.at[2])
    wide = identity(BLOCK)
    for h in range(2):
        await_bytes(f_recv.at[h], f_sem.at[2 + h])
        for m in range(nm):
            parts = [f_recv[h, zh, m * YLO * ZLO : (m + 1) * YLO * ZLO, :].astype(F32) for zh in range(ny_dev)]
            rows = [parts[zh][y * ZLO : (y + 1) * ZLO] for y in range(YLO) for zh in range(ny_dev)]
            tile = jnp.concatenate(rows, axis=0).astype(BF16)
            out[h * BLOCK : (h + 1) * BLOCK, m * chunk : (m + 1) * chunk] = nt(wide, tile).astype(BF16)
    for h in range(2):
        await_bytes(f_send.at[h, pl.ds(0, ny_dev - 1)], f_sem.at[h])


def local(dims, source, prior, coupling, pairs, transmission, direction):
    nm, ny_dev, nz_dev, ny, nz = dims
    modes = source.shape[0]
    group = nm * ny_dev
    chunk = YLO * nz
    tall = ny * ZLO
    per_z = tall // nz_dev
    vmem = pl.BlockSpec(memory_space=pltpu.VMEM)
    hbm = pl.BlockSpec(memory_space=pltpu.HBM)
    dma = pltpu.SemaphoreType.DMA
    result = pl.pallas_call(
        functools.partial(kernel, dims),
        out_shape=jax.ShapeDtypeStruct((modes, ny * nz), BF16),
        in_specs=[hbm] * 6,
        out_specs=vmem,
        scratch_shapes=[
            pltpu.SMEM((PER_ROW, 2 * nm), jnp.int32),
            pltpu.VMEM((3, modes), F32),
            pltpu.VMEM((3, modes), jnp.int32),
            pltpu.VMEM((modes, ny * nz), BF16),
            pltpu.VMEM((modes, ny * nz), BF16),
            pltpu.VMEM((2, nm, chunk, BLOCK), BF16),
            pltpu.VMEM((2, nm, chunk, BLOCK), BF16),
            pltpu.VMEM((nm, 2, chunk, BLOCK), BF16),
            pltpu.VMEM((ny_dev, 2, tall, BLOCK), I16),
            pltpu.VMEM((ny_dev, 2, tall, BLOCK), I16),
            pltpu.VMEM((nm, 1, BLOCK), F32),
            pltpu.VMEM((ny_dev, nm, 1, BLOCK), F32),
            pltpu.VMEM((nm, 2 * PER_ROW, BLOCK, BLOCK), BF16),
            pltpu.VMEM((2, 8, BLOCK), F32),
            pltpu.VMEM((nm, 2, 8, BLOCK), F32),
            pltpu.VMEM((2 * chunk, BLOCK), F32),
            pltpu.VMEM((2, group, YLO * ZLO, BLOCK), I16),
            pltpu.VMEM((2, group, YLO * ZLO, BLOCK), I16),
            pltpu.VMEM((nm, 1, BLOCK), F32),
            pltpu.VMEM((group, 1, BLOCK), F32),
            pltpu.VMEM((2, XLO, tall, BLOCK), F32),
            pltpu.VMEM((2, tall, BLOCK), F32),
            pltpu.VMEM((2, nz_dev, per_z, BLOCK), I16),
            pltpu.VMEM((2, nz_dev, per_z, BLOCK), I16),
            pltpu.VMEM((2, 1, BLOCK), F32),
            pltpu.VMEM((2, nz_dev, 1, BLOCK), F32),
            pltpu.VMEM((2, nz_dev, per_z, BLOCK), I16),
            pltpu.VMEM((2, nz_dev, per_z, BLOCK), I16),
            pltpu.VMEM((2, 1, BLOCK), F32),
            pltpu.VMEM((2, nz_dev, 1, BLOCK), F32),
            pltpu.VMEM((2, group, YLO * ZLO, BLOCK), BF16),
            pltpu.VMEM((2, ny_dev, tall, BLOCK), BF16),
            pltpu.VMEM((2, ny_dev, tall, BLOCK), BF16),
            pltpu.SemaphoreType.REGULAR((4,)),
            dma((6,)),
            dma((4,)),
            dma((4,)),
            dma((5,)),
            dma((2,)),
            dma((nm // 2,)),
            dma((nm // 2,)),
            dma((4,)),
            dma((4,)),
            dma((4,)),
            dma((4,)),
            dma((4,)),
            dma((10,)),
        ],
        compiler_params=pltpu.CompilerParams(
            collective_id=0, has_side_effects=True, vmem_limit_bytes=60 * 1024 * 1024
        ),
        cost_estimate=pl.CostEstimate(flops=600_000_000, bytes_accessed=2_000_000, transcendentals=0),
    )(
        source.reshape(modes, ny * nz),
        prior.reshape(modes, ny * nz),
        coupling.reshape(2 * PER_ROW, BLOCK, BLOCK),
        pairs.T,
        transmission,
        direction,
    )
    return result.reshape(modes, 1, ny * nz)


def build(mesh, ny, nz):
    nm = mesh.shape["mode"]
    ny_dev = nz // ZLO
    nz_dev = mesh.shape["cell"] // ny_dev
    in_specs = (
        P("mode", "cell", None),
        P("mode", "cell", None),
        P("mode", None, None, None),
        P(),
        P(None, "mode"),
        P(None, "mode"),
    )
    body = functools.partial(local, (nm, ny_dev, nz_dev, ny, nz))
    return jax.shard_map(body, mesh=mesh, in_specs=in_specs, out_specs=P("mode", "cell", None), check_vma=False)


def solution(mesh):
    return build(mesh, 32, 32)
```

```python
import functools

import jax
import jax.numpy as jnp
from jax import lax
from jax.experimental import pallas as pl
from jax.experimental.pallas import tpu as pltpu
from jax.sharding import PartitionSpec as P

ITERS = 2
BLOCK = 128
PER_ROW = 4
ZLO = 8
YLO = 4
XLO = 4
TOP = 32767.0
F32 = jnp.float32
BF16 = jnp.bfloat16
I16 = jnp.int16
MESH = pl.DeviceIdType.MESH


def nt(left, right):
    return lax.dot_general(left, right, (((1,), (1,)), ((), ())), preferred_element_type=F32)


def identity(size):
    rows = lax.broadcasted_iota(jnp.int32, (size, size), 0)
    columns = lax.broadcasted_iota(jnp.int32, (size, size), 1)
    return jnp.where(rows == columns, 1.0, 0.0).astype(BF16)


def run(values, factor, forward):
    n = len(values)
    ordered = [jnp.where(forward, values[s], values[n - 1 - s]) for s in range(n)]
    swept = [ordered[0]]
    for s in range(1, n):
        swept.append(factor * swept[-1] + ordered[s])
    return [jnp.where(forward, swept[s], swept[n - 1 - s]) for s in range(n)]


def farthest_first(j, n):
    if isinstance(j, int):
        return (n // 2 + (j // 2 if j % 2 == 0 else -((j + 1) // 2))) % n
    return n // 2 + jnp.where(j % 2 == 0, j // 2, -((j + 1) // 2)) + n


def encode(values, scale):
    return jnp.round(values * scale).astype(jnp.int32).astype(I16)


def decode(codes):
    return codes.astype(jnp.int32).astype(F32)


def kernel(
    dims,
    source,
    prior,
    coupling,
    pairs_in,
    transmission_in,
    direction_in,
    out,
    pairs,
    transmission,
    direction,
    source_v,
    prior_v,
    cur_a,
    cur_b,
    turned,
    s_send,
    s_recv,
    ss_send,
    ss_recv,
    blocks,
    coef_own,
    coef,
    work,
    x_send,
    x_recv,
    xs_send,
    xs_recv,
    planes,
    ends,
    e_send,
    e_recv,
    es_send,
    es_recv,
    b_send,
    b_recv,
    bs_send,
    bs_recv,
    c_send,
    f_send,
    f_recv,
    round_sem,
    in_sem,
    s0_send,
    s0_recv,
    gather_send,
    gather_recv,
    direct_sem,
    part_sem,
    x_sem,
    e_sem,
    b_sem,
    c_sem,
    f_sem,
    scale_sem,
):
    nm, ny_dev, nz_dev, ny, nz = dims
    chips = nm // 2
    chunk = YLO * nz
    tall = ny * ZLO
    per_z = tall // nz_dev
    me_m = lax.axis_index("mode")
    me_c = lax.axis_index("cell")
    me_z, me_y = me_c // ny_dev, me_c % ny_dev
    me_x, me_core = me_m // 2, me_m % 2

    def remote(src, dst, send, recv, to):
        return pltpu.make_async_remote_copy(
            src_ref=src, dst_ref=dst, send_sem=send, recv_sem=recv, device_id=to, device_id_type=MESH
        )

    def mode_at(j):
        x = (me_x + farthest_first(j // 2, chips)) % chips
        return x * 2 + (me_core + 1 + j % 2) % 2

    def y_at(i):
        return (me_y + farthest_first(i, ny_dev)) % ny_dev

    def await_bytes(ref, sem):
        pltpu.make_async_copy(ref, ref, sem).wait()

    loads = [
        pltpu.make_async_copy(prior, prior_v, in_sem.at[0]),
        pltpu.make_async_copy(coupling, blocks.at[me_m], in_sem.at[1]),
        pltpu.make_async_copy(source, source_v, in_sem.at[2]),
    ]
    small = [
        pltpu.make_async_copy(transmission_in, transmission, in_sem.at[3]),
        pltpu.make_async_copy(direction_in, direction, in_sem.at[4]),
        pltpu.make_async_copy(pairs_in, pairs, in_sem.at[5]),
    ]

    barrier = pltpu.get_barrier_semaphore()
    group = nm * ny_dev
    near = [(me_z * ny_dev + (me_y + i) % ny_dev, me_m) for i in range(1, ny_dev)]
    near += [(me_c, (me_m + j) % nm) for j in range(1, nm)]

    def ring(step):
        return [((me_z + z) % nz_dev * ny_dev + me_y, me_m) for z in sorted({step % nz_dev, -step % nz_dev} - {0})]

    near += ring(1)
    for to in near:
        pl.semaphore_signal(barrier, inc=1, device_id=to, device_id_type=MESH)
    for load in small + loads:
        load.start()

    rounds = []
    while 2 ** len(rounds) < nz_dev // 2:
        rounds.append(2 ** len(rounds))

    def meet(r):
        if r and r - 1 < len(rounds):
            pl.semaphore_wait(round_sem.at[r - 1], 2)
        if r < len(rounds):
            for to in ring(rounds[r]):
                pl.semaphore_signal(round_sem.at[r], inc=1, device_id=to, device_id_type=MESH)

    for load in small:
        load.wait()
    fwd = {}
    fac = {}
    weight = {}
    for h in range(2):
        lanes = slice(h * BLOCK, (h + 1) * BLOCK)
        for d in range(3):
            fac[d, h] = jnp.broadcast_to(transmission[d : d + 1, lanes], (8, BLOCK))
            fwd[d, h] = jnp.broadcast_to(direction[d : d + 1, lanes], (8, BLOCK)) == 1
        total = jnp.sqrt(1.0 - transmission[0:1, lanes] * transmission[0:1, lanes])
        for d in range(1, 3):
            total = total * jnp.sqrt(1.0 - transmission[d : d + 1, lanes] * transmission[d : d + 1, lanes])
        weight[h] = total
    for h in range(2):
        coef_own[0, h * 4 : h * 4 + 4, :] = fac[2, h][:4]
        coef_own[1, h * 4 : h * 4 + 4, :] = jnp.where(fwd[2, h], 1.0, 0.0)[:4]

    eye = identity(chunk)

    loads[0].wait()
    for m in range(nm):
        for h in range(2):
            tile = nt(eye, prior_v[h * BLOCK : (h + 1) * BLOCK, m * chunk : (m + 1) * chunk])
            rows = [
                tile[y * nz + zh * ZLO : y * nz + (zh + 1) * ZLO] for zh in range(ny_dev) for y in range(YLO)
            ]
            turned[m, h] = jnp.concatenate(rows, axis=0).astype(BF16)

    def sweep_z(factor, forward):
        values = run([work[pl.ds(z, 8, stride=nz), :] for z in range(nz)], factor, forward)
        largest = jnp.abs(values[0])
        for z in range(nz):
            work[pl.ds(z, 8, stride=nz), :] = values[z]
            if z:
                largest = jnp.maximum(largest, jnp.abs(values[z]))
        largest = jnp.maximum(jnp.max(largest, axis=0, keepdims=True), 1e-30)
        return TOP / largest, largest * (1.0 / TOP)

    def two_rows(h, y, zh):
        start = h * chunk + y * nz + zh * ZLO
        return jnp.concatenate([work[start : start + ZLO, :], work[start + nz : start + nz + ZLO, :]], axis=0)

    loads[1].wait()
    pl.semaphore_wait(barrier, len(near))
    meet(0)

    sibling = me_x * 2 + 1 - me_core
    shared = pl.ds(PER_ROW + me_y, 1)
    direct = pl.ds(0, PER_ROW)
    for j in [farthest_first(i, chips) for i in range(chips - 1)]:
        to = (me_c, ((me_x + j) % chips) * 2 + me_core)
        part = blocks.at[me_m, shared]
        remote(part, part, gather_send.at[0], part_sem.at[j], to).start()
    pltpu.make_async_copy(turned.at[me_m], cur_a.at[:, me_m], s0_recv.at[0]).start()
    for j in range(nm - 1):
        m = mode_at(j)
        remote(turned.at[m], cur_a.at[:, me_m], s0_send.at[0], s0_recv.at[0], (me_c, m)).start()
    pltpu.make_async_copy(coef_own, coef.at[me_m], s0_recv.at[2]).start()
    for j in range(nm - 1):
        m = mode_at(j)
        remote(coef_own, coef.at[me_m], s0_send.at[2], s0_recv.at[2], (me_c, m)).start()
    for j in [farthest_first(i, chips) for i in range(chips - 1)]:
        to = (me_c, ((me_x + j) % chips) * 2 + me_core)
        part = blocks.at[me_m, direct]
        remote(part, part, gather_send.at[1], direct_sem.at[j], to).start()
    own = blocks.at[me_m]
    remote(own, own, gather_send.at[2], gather_recv.at[1], (me_c, sibling)).start()

    def over_y(m):
        part = blocks.at[m, shared]
        for i in range(ny_dev - 1):
            to = (me_z * ny_dev + y_at(i), me_m)
            remote(part, part, gather_send.at[3], gather_recv.at[0], to).start()

    meet(1)
    for j in [farthest_first(i, chips) for i in range(chips - 1)]:
        m = ((me_x + chips - j) % chips) * 2 + me_core
        await_bytes(blocks.at[m, shared], part_sem.at[j])
        over_y(m)

    meet(2)
    loads[2].wait()

    def sweep_source(m, carry):
        for h in range(2):
            columns = pl.ds(pl.multiple_of(m * chunk, chunk), chunk)
            work[h * chunk : (h + 1) * chunk, :] = nt(eye, source_v[h * BLOCK : (h + 1) * BLOCK, columns])
        scale, unit = sweep_z(coef_own[0], coef_own[1] > 0.5)
        ss_send[m] = unit
        for zh in range(ny_dev):
            for h in range(2):
                for y in range(0, YLO, 2):
                    rows = pl.ds(m * YLO * ZLO + y * ZLO, 2 * ZLO)
                    s_send[zh, h, rows, :] = encode(two_rows(h, y, zh), scale)
        return carry

    lax.fori_loop(0, nm, sweep_source, 0)
    for i in range(ny_dev - 1):
        y = y_at(i)
        to = (me_z * ny_dev + y, me_m)
        remote(s_send.at[y], s_recv.at[me_y], s0_send.at[1], s0_recv.at[1], to).start()
        remote(ss_send, ss_recv.at[me_y], s0_send.at[3], s0_recv.at[3], to).start()
    pltpu.make_async_copy(s_send.at[me_y], s_recv.at[me_y], s0_recv.at[1]).start()
    pltpu.make_async_copy(ss_send, ss_recv.at[me_y], s0_recv.at[3]).start()
    for j in range(1, chips):
        part = blocks.at[((me_x + chips - j) % chips) * 2 + me_core, direct]
        await_bytes(part, direct_sem.at[j])
        remote(part, part, gather_send.at[4], gather_recv.at[1], (me_c, sibling)).start()
    if chips > 1:
        await_bytes(blocks.at[pl.ds(0, chips - 1), pl.ds(0, ny_dev - 1)], gather_recv.at[0])
    for j in range(1, chips):
        part = blocks.at[((me_x + chips - j) % chips) * 2 + me_core, pl.ds(PER_ROW, PER_ROW)]
        remote(part, part, gather_send.at[4], gather_recv.at[1], (me_c, sibling)).start()
    meet(3)
    await_bytes(cur_a, s0_recv.at[0])
    await_bytes(coef, s0_recv.at[2])
    await_bytes(blocks.at[pl.ds(0, chips)], gather_recv.at[1])

    for iteration in range(ITERS):
        current = cur_a if iteration == 0 else cur_b
        last = iteration == ITERS - 1

        def scatter(j, carry):
            m = mode_at(j)
            for h in range(2):
                row = m * 2 + h
                left = jnp.concatenate([current[pairs[k, row] % 2, pairs[k, row] // 2] for k in range(PER_ROW)], axis=1)
                right = jnp.concatenate([blocks[m, h * PER_ROW + k] for k in range(PER_ROW)], axis=1)
                total = nt(left, right)
                for zh in range(ny_dev):
                    for y in range(YLO):
                        work[h * chunk + y * nz + zh * ZLO : h * chunk + y * nz + (zh + 1) * ZLO, :] = total[
                            (zh * YLO + y) * ZLO : (zh * YLO + y + 1) * ZLO
                        ]
            scale, unit = sweep_z(coef[m, 0], coef[m, 1] > 0.5)
            xs_send[m] = unit
            for zh in range(ny_dev):
                for h in range(2):
                    for y in range(0, YLO, 2):
                        x_send[h, m * ny_dev + zh, y * ZLO : (y + 2) * ZLO, :] = encode(two_rows(h, y, zh), scale)
            send_codes(j, 0, True)
            return carry

        def send_codes(j, h, with_scale):
            m = mode_at(j)
            slot = me_m * ny_dev + me_y
            for i in range(ny_dev):
                y = y_at(i)
                to = (me_z * ny_dev + y, m)

                def send():
                    src, dst = x_send.at[h, m * ny_dev + y], x_recv.at[h, slot]
                    remote(src, dst, x_sem.at[h], x_sem.at[2 + h], to).start()
                    if with_scale:
                        remote(xs_send.at[m], xs_recv.at[slot], scale_sem.at[0], scale_sem.at[1], to).start()

                def keep():
                    src, dst = x_send.at[h, m * ny_dev + y], x_recv.at[h, slot]
                    pltpu.make_async_copy(src, dst, x_sem.at[2 + h]).start()
                    if with_scale:
                        pltpu.make_async_copy(xs_send.at[m], xs_recv.at[slot], scale_sem.at[1]).start()

                if i < ny_dev - 1:
                    send()
                else:
                    pl.when(j < nm - 1)(send)
                    pl.when(j == nm - 1)(keep)

        def send_second(j, carry):
            send_codes(j, 1, False)
            return carry

        lax.fori_loop(0, nm, scatter, 0)
        lax.fori_loop(0, nm, send_second, 0)

        def send_ring(h, scale, codes, into, sem, unit, units, unit_sem):
            def one(j, carry):
                z = (me_z + farthest_first(j, nz_dev)) % nz_dev
                codes[h, z] = encode(ends[h, pl.ds(z * per_z, per_z), :], scale)
                to = (z * ny_dev + me_y, me_m)

                @pl.when(j < nz_dev - 1)
                def _():
                    remote(codes.at[h, z], into.at[h, me_z], sem.at[h], sem.at[2 + h], to).start()
                    remote(
                        unit.at[h], units.at[h, me_z], scale_sem.at[unit_sem + h], scale_sem.at[unit_sem + 2 + h], to
                    ).start()

                @pl.when(j == nz_dev - 1)
                def _():
                    pltpu.make_async_copy(codes.at[h, z], into.at[h, me_z], sem.at[2 + h]).start()
                    pltpu.make_async_copy(unit.at[h], units.at[h, me_z], scale_sem.at[unit_sem + 2 + h]).start()

                return carry

            lax.fori_loop(0, nz_dev, one, 0)

        def wide_fac(h):
            return jnp.concatenate([fac[0, h]] * YLO, axis=0)

        def wide_fwd(h):
            tile = jnp.broadcast_to(direction[0:1, h * BLOCK : (h + 1) * BLOCK], (8, BLOCK))
            return jnp.concatenate([tile] * YLO, axis=0) == 1

        def hand_on(h):
            def unpack(m, carry):
                rows = pl.ds(m * YLO * ZLO, YLO * ZLO)
                got = []
                for x in range(XLO):
                    value = decode(x_recv[h, m * ny_dev + x]) * (xs_recv[m * ny_dev + x] * weight[h])
                    value += decode(s_recv[x, h, rows, :]) * (ss_recv[x, m] * weight[h])
                    planes[h, x, rows, :] = value
                    got.append(value)
                t, f = wide_fac(h), wide_fwd(h)
                end = jnp.where(f, got[0], got[XLO - 1])
                for x in range(1, XLO):
                    end = end * t + jnp.where(f, got[x], got[XLO - 1 - x])
                ends[h, rows, :] = end
                return carry

            lax.fori_loop(0, nm, unpack, 0)
            values = [ends[h, y * ZLO : (y + 1) * ZLO, :] for y in range(ny)]
            values = run(values, fac[1, h], fwd[1, h])
            largest = jnp.full((8, BLOCK), 1e-30, F32)
            for y in range(ny):
                ends[h, y * ZLO : (y + 1) * ZLO, :] = values[y]
                largest = jnp.maximum(largest, jnp.abs(values[y]))
            largest = jnp.max(largest, axis=0, keepdims=True)
            es_send[h] = largest * (1.0 / TOP)
            send_ring(h, TOP / largest, e_send, e_recv, e_sem, es_send, es_recv, 2)

        def sweep_y(h):
            def one(x, carry):
                values = [planes[h, x, y * ZLO : (y + 1) * ZLO, :] for y in range(ny)]
                values = run(values, fac[1, h], fwd[1, h])
                for y in range(ny):
                    planes[h, x, y * ZLO : (y + 1) * ZLO, :] = values[y]
                return carry

            lax.fori_loop(0, XLO, one, 0)

        def scan_ring(h):
            largest = jnp.full((8, BLOCK), 1e-30, F32)
            leap = fac[0, h] * fac[0, h]
            leap = leap * leap
            f = fwd[0, h]
            for part in range(per_z // 16):
                got = [
                    decode(e_recv[h, z, part * 16 : part * 16 + 16, :]) * es_recv[h, z] for z in range(nz_dev)
                ]
                for i in range(2):
                    given = [g[i * 8 : i * 8 + 8] for g in got]
                    ordered = [jnp.where(f, given[s], given[nz_dev - 1 - s]) for s in range(nz_dev)]
                    taken = [jnp.zeros_like(ordered[0])]
                    for s in range(nz_dev - 1):
                        taken.append(leap * taken[-1] + ordered[s])
                    for z in range(nz_dev):
                        value = jnp.where(f, taken[z], taken[nz_dev - 1 - z])
                        start = z * per_z + part * 16 + i * 8
                        ends[h, start : start + 8, :] = value
                        largest = jnp.maximum(largest, jnp.abs(value))
            largest = jnp.max(largest, axis=0, keepdims=True)
            bs_send[h] = largest * (1.0 / TOP)
            send_ring(h, TOP / largest, b_send, b_recv, b_sem, bs_send, bs_recv, 6)

        def finish_half(h):
            def inflow(z, carry):
                ends[h, pl.ds(z * per_z, per_z), :] = decode(b_recv[h, z]) * bs_recv[h, z]
                return carry

            lax.fori_loop(0, nz_dev, inflow, 0)

            def finish(j, carry):
                m = mode_at(j)
                rows = pl.ds(m * YLO * ZLO, YLO * ZLO)
                t, f = wide_fac(h), wide_fwd(h)
                given = [planes[h, x, rows, :] for x in range(XLO)]
                value = ends[h, rows, :]
                swept = []
                for x in range(XLO):
                    value = t * value + jnp.where(f, given[x], given[XLO - 1 - x])
                    swept.append(value)
                for x in range(XLO):
                    result = jnp.where(f, swept[x], swept[XLO - 1 - x]).astype(BF16)
                    if last:
                        f_send[h, x, rows, :] = result
                    else:
                        c_send[h, m * ny_dev + x] = result
                if not last:
                    for i in range(ny_dev):
                        y = y_at(i)
                        to = (me_z * ny_dev + y, m)
                        into = cur_b.at[h, me_m, pl.ds(me_y * YLO * ZLO, YLO * ZLO), :]

                        def send():
                            remote(c_send.at[h, m * ny_dev + y], into, c_sem.at[h], c_sem.at[2 + h], to).start()

                        def keep():
                            pltpu.make_async_copy(c_send.at[h, m * ny_dev + y], into, c_sem.at[2 + h]).start()

                        if i < ny_dev - 1:
                            send()
                        else:
                            pl.when(j < nm - 1)(send)
                            pl.when(j == nm - 1)(keep)
                return carry

            lax.fori_loop(0, nm, finish, 0)
            if last:
                for i in range(ny_dev - 1):
                    y = y_at(i)
                    to = (me_z * ny_dev + y, me_m)
                    remote(f_send.at[h, y], f_recv.at[h, me_y], f_sem.at[h], f_sem.at[2 + h], to).start()
                pltpu.make_async_copy(f_send.at[h, me_y], f_recv.at[h, me_y], f_sem.at[2 + h]).start()

        await_bytes(x_recv.at[0], x_sem.at[2])
        await_bytes(xs_recv, scale_sem.at[1])
        if iteration == 0:
            await_bytes(s_recv, s0_recv.at[1])
            await_bytes(ss_recv, s0_recv.at[3])
        hand_on(0)
        await_bytes(x_recv.at[1], x_sem.at[3])
        hand_on(1)
        sweep_y(0)
        for h in range(2):
            await_bytes(e_recv.at[h], e_sem.at[2 + h])
            await_bytes(es_recv.at[h], scale_sem.at[4 + h])
            scan_ring(h)
            if h == 0:
                sweep_y(1)
        for h in range(2):
            await_bytes(b_recv.at[h], b_sem.at[2 + h])
            await_bytes(bs_recv.at[h], scale_sem.at[8 + h])
            finish_half(h)
        await_bytes(xs_recv.at[pl.ds(0, group - 1)], scale_sem.at[0])
        for h in range(2):
            await_bytes(x_send.at[h, pl.ds(0, group - 1)], x_sem.at[h])
            await_bytes(e_send.at[h, pl.ds(0, nz_dev - 1)], e_sem.at[h])
            await_bytes(es_recv.at[h, pl.ds(0, nz_dev - 1)], scale_sem.at[2 + h])
            await_bytes(b_send.at[h, pl.ds(0, nz_dev - 1)], b_sem.at[h])
            await_bytes(bs_recv.at[h, pl.ds(0, nz_dev - 1)], scale_sem.at[6 + h])
        if not last:
            for h in range(2):
                await_bytes(cur_b.at[h], c_sem.at[2 + h])
                await_bytes(c_send.at[h, pl.ds(0, group - 1)], c_sem.at[h])

    await_bytes(turned.at[pl.ds(0, nm - 1)], s0_send.at[0])
    await_bytes(s_send.at[pl.ds(0, ny_dev - 1)], s0_send.at[1])
    await_bytes(ss_recv.at[pl.ds(0, ny_dev - 1)], s0_send.at[3])
    await_bytes(coef.at[pl.ds(0, nm - 1)], s0_send.at[2])
    if chips > 1:
        await_bytes(blocks.at[0, pl.ds(0, chips - 1)], gather_send.at[0])
        await_bytes(blocks.at[pl.ds(0, chips - 1), direct], gather_send.at[1])
        await_bytes(blocks.at[pl.ds(0, chips - 1), pl.ds(0, ny_dev - 1)], gather_send.at[3])
        await_bytes(blocks.at[pl.ds(0, chips - 1)], gather_send.at[4])
    await_bytes(blocks.at[0], gather_send.at[2])
    wide = identity(BLOCK)
    for h in range(2):
        await_bytes(f_recv.at[h], f_sem.at[2 + h])
        for m in range(nm):
            parts = [f_recv[h, zh, m * YLO * ZLO : (m + 1) * YLO * ZLO, :].astype(F32) for zh in range(ny_dev)]
            rows = [parts[zh][y * ZLO : (y + 1) * ZLO] for y in range(YLO) for zh in range(ny_dev)]
            tile = jnp.concatenate(rows, axis=0).astype(BF16)
            out[h * BLOCK : (h + 1) * BLOCK, m * chunk : (m + 1) * chunk] = nt(wide, tile).astype(BF16)
    for h in range(2):
        await_bytes(f_send.at[h, pl.ds(0, ny_dev - 1)], f_sem.at[h])


def local(dims, source, prior, coupling, pairs, transmission, direction):
    nm, ny_dev, nz_dev, ny, nz = dims
    modes = source.shape[0]
    group = nm * ny_dev
    chunk = YLO * nz
    tall = ny * ZLO
    per_z = tall // nz_dev
    vmem = pl.BlockSpec(memory_space=pltpu.VMEM)
    hbm = pl.BlockSpec(memory_space=pltpu.HBM)
    dma = pltpu.SemaphoreType.DMA
    result = pl.pallas_call(
        functools.partial(kernel, dims),
        out_shape=jax.ShapeDtypeStruct((modes, ny * nz), BF16),
        in_specs=[hbm] * 6,
        out_specs=vmem,
        scratch_shapes=[
            pltpu.SMEM((PER_ROW, 2 * nm), jnp.int32),
            pltpu.VMEM((3, modes), F32),
            pltpu.VMEM((3, modes), jnp.int32),
            pltpu.VMEM((modes, ny * nz), BF16),
            pltpu.VMEM((modes, ny * nz), BF16),
            pltpu.VMEM((2, nm, chunk, BLOCK), BF16),
            pltpu.VMEM((2, nm, chunk, BLOCK), BF16),
            pltpu.VMEM((nm, 2, chunk, BLOCK), BF16),
            pltpu.VMEM((ny_dev, 2, tall, BLOCK), I16),
            pltpu.VMEM((ny_dev, 2, tall, BLOCK), I16),
            pltpu.VMEM((nm, 1, BLOCK), F32),
            pltpu.VMEM((ny_dev, nm, 1, BLOCK), F32),
            pltpu.VMEM((nm, 2 * PER_ROW, BLOCK, BLOCK), BF16),
            pltpu.VMEM((2, 8, BLOCK), F32),
            pltpu.VMEM((nm, 2, 8, BLOCK), F32),
            pltpu.VMEM((2 * chunk, BLOCK), F32),
            pltpu.VMEM((2, group, YLO * ZLO, BLOCK), I16),
            pltpu.VMEM((2, group, YLO * ZLO, BLOCK), I16),
            pltpu.VMEM((nm, 1, BLOCK), F32),
            pltpu.VMEM((group, 1, BLOCK), F32),
            pltpu.VMEM((2, XLO, tall, BLOCK), F32),
            pltpu.VMEM((2, tall, BLOCK), F32),
            pltpu.VMEM((2, nz_dev, per_z, BLOCK), I16),
            pltpu.VMEM((2, nz_dev, per_z, BLOCK), I16),
            pltpu.VMEM((2, 1, BLOCK), F32),
            pltpu.VMEM((2, nz_dev, 1, BLOCK), F32),
            pltpu.VMEM((2, nz_dev, per_z, BLOCK), I16),
            pltpu.VMEM((2, nz_dev, per_z, BLOCK), I16),
            pltpu.VMEM((2, 1, BLOCK), F32),
            pltpu.VMEM((2, nz_dev, 1, BLOCK), F32),
            pltpu.VMEM((2, group, YLO * ZLO, BLOCK), BF16),
            pltpu.VMEM((2, ny_dev, tall, BLOCK), BF16),
            pltpu.VMEM((2, ny_dev, tall, BLOCK), BF16),
            pltpu.SemaphoreType.REGULAR((4,)),
            dma((6,)),
            dma((4,)),
            dma((4,)),
            dma((5,)),
            dma((2,)),
            dma((nm // 2,)),
            dma((nm // 2,)),
            dma((4,)),
            dma((4,)),
            dma((4,)),
            dma((4,)),
            dma((4,)),
            dma((10,)),
        ],
        compiler_params=pltpu.CompilerParams(
            collective_id=0, has_side_effects=True, vmem_limit_bytes=60 * 1024 * 1024
        ),
        cost_estimate=pl.CostEstimate(flops=600_000_000, bytes_accessed=2_000_000, transcendentals=0),
    )(
        source.reshape(modes, ny * nz),
        prior.reshape(modes, ny * nz),
        coupling.reshape(2 * PER_ROW, BLOCK, BLOCK),
        pairs.T,
        transmission,
        direction,
    )
    return result.reshape(modes, 1, ny * nz)


def build(mesh, ny, nz):
    nm = mesh.shape["mode"]
    ny_dev = nz // ZLO
    nz_dev = mesh.shape["cell"] // ny_dev
    in_specs = (
        P("mode", "cell", None),
        P("mode", "cell", None),
        P("mode", None, None, None),
        P(),
        P(None, "mode"),
        P(None, "mode"),
    )
    body = functools.partial(local, (nm, ny_dev, nz_dev, ny, nz))
    return jax.shard_map(body, mesh=mesh, in_specs=in_specs, out_specs=P("mode", "cell", None), check_vma=False)


def solution(mesh):
    return build(mesh, 32, 32)
```

```python
import functools

import jax
import jax.numpy as jnp
from jax import lax
from jax.experimental import pallas as pl
from jax.experimental.pallas import tpu as pltpu
from jax.sharding import PartitionSpec as P

ITERS = 2
BLOCK = 128
PER_ROW = 4
ZLO = 8
YLO = 4
XLO = 4
TOP = 32767.0
F32 = jnp.float32
BF16 = jnp.bfloat16
I16 = jnp.int16
MESH = pl.DeviceIdType.MESH


def nt(left, right):
    return lax.dot_general(left, right, (((1,), (1,)), ((), ())), preferred_element_type=F32)


def identity(size):
    rows = lax.broadcasted_iota(jnp.int32, (size, size), 0)
    columns = lax.broadcasted_iota(jnp.int32, (size, size), 1)
    return jnp.where(rows == columns, 1.0, 0.0).astype(BF16)


def run(values, factor, forward):
    n = len(values)
    ordered = [jnp.where(forward, values[s], values[n - 1 - s]) for s in range(n)]
    swept = [ordered[0]]
    for s in range(1, n):
        swept.append(factor * swept[-1] + ordered[s])
    return [jnp.where(forward, swept[s], swept[n - 1 - s]) for s in range(n)]


def farthest_first(j, n):
    if isinstance(j, int):
        return (n // 2 + (j // 2 if j % 2 == 0 else -((j + 1) // 2))) % n
    return n // 2 + jnp.where(j % 2 == 0, j // 2, -((j + 1) // 2)) + n


def encode(values, scale):
    return jnp.round(values * scale).astype(jnp.int32).astype(I16)


def decode(codes):
    return codes.astype(jnp.int32).astype(F32)


def kernel(
    dims,
    source,
    prior,
    coupling,
    pairs_in,
    transmission_in,
    direction_in,
    out,
    pairs,
    transmission,
    direction,
    source_v,
    prior_v,
    cur_a,
    cur_b,
    turned,
    s_send,
    s_recv,
    ss_send,
    ss_recv,
    blocks,
    coef_own,
    coef,
    work,
    x_send,
    x_recv,
    xs_send,
    xs_recv,
    planes,
    ends,
    e_send,
    e_recv,
    es_send,
    es_recv,
    b_send,
    b_recv,
    bound,
    c_send,
    f_send,
    f_recv,
    round_sem,
    in_sem,
    s0_send,
    s0_recv,
    gather_send,
    gather_recv,
    direct_sem,
    part_sem,
    x_sem,
    e_sem,
    b_sem,
    c_sem,
    f_sem,
    scale_sem,
):
    nm, ny_dev, nz_dev, ny, nz = dims
    chips = nm // 2
    chunk = YLO * nz
    tall = ny * ZLO
    per_z = tall // nz_dev
    me_m = lax.axis_index("mode")
    me_c = lax.axis_index("cell")
    me_z, me_y = me_c // ny_dev, me_c % ny_dev
    me_x, me_core = me_m // 2, me_m % 2

    def remote(src, dst, send, recv, to):
        return pltpu.make_async_remote_copy(
            src_ref=src, dst_ref=dst, send_sem=send, recv_sem=recv, device_id=to, device_id_type=MESH
        )

    def mode_at(j):
        x = (me_x + farthest_first(j // 2, chips)) % chips
        return x * 2 + (me_core + 1 + j % 2) % 2

    def y_at(i):
        return (me_y + farthest_first(i, ny_dev)) % ny_dev

    def await_bytes(ref, sem):
        pltpu.make_async_copy(ref, ref, sem).wait()

    loads = [
        pltpu.make_async_copy(prior, prior_v, in_sem.at[0]),
        pltpu.make_async_copy(coupling, blocks.at[me_m], in_sem.at[1]),
        pltpu.make_async_copy(source, source_v, in_sem.at[2]),
    ]
    small = [
        pltpu.make_async_copy(transmission_in, transmission, in_sem.at[3]),
        pltpu.make_async_copy(direction_in, direction, in_sem.at[4]),
        pltpu.make_async_copy(pairs_in, pairs, in_sem.at[5]),
    ]

    barrier = pltpu.get_barrier_semaphore()
    group = nm * ny_dev
    near = [(me_z * ny_dev + (me_y + i) % ny_dev, me_m) for i in range(1, ny_dev)]
    near += [(me_c, (me_m + j) % nm) for j in range(1, nm)]

    def ring(step):
        return [((me_z + z) % nz_dev * ny_dev + me_y, me_m) for z in sorted({step % nz_dev, -step % nz_dev} - {0})]

    near += ring(1)
    for to in near:
        pl.semaphore_signal(barrier, inc=1, device_id=to, device_id_type=MESH)
    for load in small + loads:
        load.start()

    rounds = []
    while 2 ** len(rounds) < nz_dev // 2:
        rounds.append(2 ** len(rounds))

    def meet(r):
        if r and r - 1 < len(rounds):
            pl.semaphore_wait(round_sem.at[r - 1], 2)
        if r < len(rounds):
            for to in ring(rounds[r]):
                pl.semaphore_signal(round_sem.at[r], inc=1, device_id=to, device_id_type=MESH)

    for load in small:
        load.wait()
    fwd = {}
    fac = {}
    weight = {}
    for h in range(2):
        lanes = slice(h * BLOCK, (h + 1) * BLOCK)
        for d in range(3):
            fac[d, h] = jnp.broadcast_to(transmission[d : d + 1, lanes], (8, BLOCK))
            fwd[d, h] = jnp.broadcast_to(direction[d : d + 1, lanes], (8, BLOCK)) == 1
        total = jnp.sqrt(1.0 - transmission[0:1, lanes] * transmission[0:1, lanes])
        for d in range(1, 3):
            total = total * jnp.sqrt(1.0 - transmission[d : d + 1, lanes] * transmission[d : d + 1, lanes])
        weight[h] = total
    for h in range(2):
        coef_own[0, h * 4 : h * 4 + 4, :] = fac[2, h][:4]
        coef_own[1, h * 4 : h * 4 + 4, :] = jnp.where(fwd[2, h], 1.0, 0.0)[:4]

    eye = identity(chunk)

    loads[0].wait()
    for m in range(nm):
        for h in range(2):
            tile = nt(eye, prior_v[h * BLOCK : (h + 1) * BLOCK, m * chunk : (m + 1) * chunk])
            rows = [
                tile[y * nz + zh * ZLO : y * nz + (zh + 1) * ZLO] for zh in range(ny_dev) for y in range(YLO)
            ]
            turned[m, h] = jnp.concatenate(rows, axis=0).astype(BF16)

    def sweep_z(factor, forward):
        values = run([work[pl.ds(z, 8, stride=nz), :] for z in range(nz)], factor, forward)
        largest = jnp.abs(values[0])
        for z in range(nz):
            work[pl.ds(z, 8, stride=nz), :] = values[z]
            if z:
                largest = jnp.maximum(largest, jnp.abs(values[z]))
        largest = jnp.maximum(jnp.max(largest, axis=0, keepdims=True), 1e-30)
        return TOP / largest, largest * (1.0 / TOP)

    def two_rows(h, y, zh):
        start = h * chunk + y * nz + zh * ZLO
        return jnp.concatenate([work[start : start + ZLO, :], work[start + nz : start + nz + ZLO, :]], axis=0)

    loads[1].wait()
    pl.semaphore_wait(barrier, len(near))
    meet(0)

    sibling = me_x * 2 + 1 - me_core
    shared = pl.ds(PER_ROW + me_y, 1)
    direct = pl.ds(0, PER_ROW)
    for j in [farthest_first(i, chips) for i in range(chips - 1)]:
        to = (me_c, ((me_x + j) % chips) * 2 + me_core)
        part = blocks.at[me_m, shared]
        remote(part, part, gather_send.at[0], part_sem.at[j], to).start()
    for j in [farthest_first(i, chips) for i in range(chips - 1)]:
        to = (me_c, ((me_x + j) % chips) * 2 + me_core)
        part = blocks.at[me_m, direct]
        remote(part, part, gather_send.at[1], direct_sem.at[j], to).start()
    pltpu.make_async_copy(turned.at[me_m], cur_a.at[:, me_m], s0_recv.at[0]).start()
    for j in range(nm - 1):
        m = mode_at(j)
        remote(turned.at[m], cur_a.at[:, me_m], s0_send.at[0], s0_recv.at[0], (me_c, m)).start()
    pltpu.make_async_copy(coef_own, coef.at[me_m], s0_recv.at[2]).start()
    for j in range(nm - 1):
        m = mode_at(j)
        remote(coef_own, coef.at[me_m], s0_send.at[2], s0_recv.at[2], (me_c, m)).start()
    own = blocks.at[me_m]
    remote(own, own, gather_send.at[2], gather_recv.at[1], (me_c, sibling)).start()

    def over_y(m):
        part = blocks.at[m, shared]
        for i in range(ny_dev - 1):
            to = (me_z * ny_dev + y_at(i), me_m)
            remote(part, part, gather_send.at[3], gather_recv.at[0], to).start()

    meet(1)
    for j in [farthest_first(i, chips) for i in range(chips - 1)]:
        m = ((me_x + chips - j) % chips) * 2 + me_core
        await_bytes(blocks.at[m, shared], part_sem.at[j])
        over_y(m)

    meet(2)
    loads[2].wait()

    def sweep_source(m, carry):
        for h in range(2):
            columns = pl.ds(pl.multiple_of(m * chunk, chunk), chunk)
            work[h * chunk : (h + 1) * chunk, :] = nt(eye, source_v[h * BLOCK : (h + 1) * BLOCK, columns])
        scale, unit = sweep_z(coef_own[0], coef_own[1] > 0.5)
        ss_send[m] = unit
        for zh in range(ny_dev):
            for h in range(2):
                for y in range(0, YLO, 2):
                    rows = pl.ds(m * YLO * ZLO + y * ZLO, 2 * ZLO)
                    s_send[zh, h, rows, :] = encode(two_rows(h, y, zh), scale)
        return carry

    lax.fori_loop(0, nm, sweep_source, 0)
    for i in range(ny_dev - 1):
        y = y_at(i)
        to = (me_z * ny_dev + y, me_m)
        remote(s_send.at[y], s_recv.at[me_y], s0_send.at[1], s0_recv.at[1], to).start()
        remote(ss_send, ss_recv.at[me_y], s0_send.at[3], s0_recv.at[3], to).start()
    pltpu.make_async_copy(s_send.at[me_y], s_recv.at[me_y], s0_recv.at[1]).start()
    pltpu.make_async_copy(ss_send, ss_recv.at[me_y], s0_recv.at[3]).start()
    for j in range(1, chips):
        part = blocks.at[((me_x + chips - j) % chips) * 2 + me_core, direct]
        await_bytes(part, direct_sem.at[j])
        remote(part, part, gather_send.at[4], gather_recv.at[1], (me_c, sibling)).start()
    if chips > 1:
        await_bytes(blocks.at[pl.ds(0, chips - 1), pl.ds(0, ny_dev - 1)], gather_recv.at[0])
    for j in range(1, chips):
        part = blocks.at[((me_x + chips - j) % chips) * 2 + me_core, pl.ds(PER_ROW, PER_ROW)]
        remote(part, part, gather_send.at[4], gather_recv.at[1], (me_c, sibling)).start()
    meet(3)
    await_bytes(cur_a, s0_recv.at[0])
    await_bytes(coef, s0_recv.at[2])
    await_bytes(blocks.at[pl.ds(0, chips)], gather_recv.at[1])

    for iteration in range(ITERS):
        current = cur_a if iteration == 0 else cur_b
        last = iteration == ITERS - 1

        def scatter(j, carry):
            m = mode_at(j)
            for h in range(2):
                row = m * 2 + h
                left = jnp.concatenate([current[pairs[k, row] % 2, pairs[k, row] // 2] for k in range(PER_ROW)], axis=1)
                right = jnp.concatenate([blocks[m, h * PER_ROW + k] for k in range(PER_ROW)], axis=1)
                total = nt(left, right)
                for zh in range(ny_dev):
                    for y in range(YLO):
                        work[h * chunk + y * nz + zh * ZLO : h * chunk + y * nz + (zh + 1) * ZLO, :] = total[
                            (zh * YLO + y) * ZLO : (zh * YLO + y + 1) * ZLO
                        ]
            scale, unit = sweep_z(coef[m, 0], coef[m, 1] > 0.5)
            xs_send[m] = unit
            for zh in range(ny_dev):
                for h in range(2):
                    for y in range(0, YLO, 2):
                        x_send[h, m * ny_dev + zh, y * ZLO : (y + 2) * ZLO, :] = encode(two_rows(h, y, zh), scale)
            send_codes(j, 0, True)
            return carry

        def send_codes(j, h, with_scale):
            m = mode_at(j)
            slot = me_m * ny_dev + me_y
            for i in range(ny_dev):
                y = y_at(i)
                to = (me_z * ny_dev + y, m)

                def send():
                    src, dst = x_send.at[h, m * ny_dev + y], x_recv.at[h, slot]
                    remote(src, dst, x_sem.at[h], x_sem.at[2 + h], to).start()
                    if with_scale:
                        remote(xs_send.at[m], xs_recv.at[slot], scale_sem.at[0], scale_sem.at[1], to).start()

                def keep():
                    src, dst = x_send.at[h, m * ny_dev + y], x_recv.at[h, slot]
                    pltpu.make_async_copy(src, dst, x_sem.at[2 + h]).start()
                    if with_scale:
                        pltpu.make_async_copy(xs_send.at[m], xs_recv.at[slot], scale_sem.at[1]).start()

                if i < ny_dev - 1:
                    send()
                else:
                    pl.when(j < nm - 1)(send)
                    pl.when(j == nm - 1)(keep)

        def send_second(j, carry):
            send_codes(j, 1, False)
            return carry

        lax.fori_loop(0, nm, scatter, 0)
        lax.fori_loop(0, nm, send_second, 0)

        def send_ring(h, scale_of, codes, into, sem, with_unit):
            def one(j, carry):
                z = (me_z + farthest_first(j, nz_dev)) % nz_dev
                codes[h, z] = encode(ends[h, pl.ds(z * per_z, per_z), :], scale_of(z))
                to = (z * ny_dev + me_y, me_m)

                @pl.when(j < nz_dev - 1)
                def _():
                    remote(codes.at[h, z], into.at[h, me_z], sem.at[h], sem.at[2 + h], to).start()
                    if with_unit:
                        remote(
                            es_send.at[h], es_recv.at[h, me_z], scale_sem.at[2 + h], scale_sem.at[4 + h], to
                        ).start()

                @pl.when(j == nz_dev - 1)
                def _():
                    pltpu.make_async_copy(codes.at[h, z], into.at[h, me_z], sem.at[2 + h]).start()
                    if with_unit:
                        pltpu.make_async_copy(es_send.at[h], es_recv.at[h, me_z], scale_sem.at[4 + h]).start()

                return carry

            lax.fori_loop(0, nz_dev, one, 0)

        def wide_fac(h):
            return jnp.concatenate([fac[0, h]] * YLO, axis=0)

        def wide_fwd(h):
            tile = jnp.broadcast_to(direction[0:1, h * BLOCK : (h + 1) * BLOCK], (8, BLOCK))
            return jnp.concatenate([tile] * YLO, axis=0) == 1

        def hand_on(h):
            def unpack(m, carry):
                rows = pl.ds(m * YLO * ZLO, YLO * ZLO)
                got = []
                for x in range(XLO):
                    value = decode(x_recv[h, m * ny_dev + x]) * (xs_recv[m * ny_dev + x] * weight[h])
                    value += decode(s_recv[x, h, rows, :]) * (ss_recv[x, m] * weight[h])
                    planes[h, x, rows, :] = value
                    got.append(value)
                t, f = wide_fac(h), wide_fwd(h)
                end = jnp.where(f, got[0], got[XLO - 1])
                for x in range(1, XLO):
                    end = end * t + jnp.where(f, got[x], got[XLO - 1 - x])
                ends[h, rows, :] = end
                return carry

            lax.fori_loop(0, nm, unpack, 0)
            values = [ends[h, y * ZLO : (y + 1) * ZLO, :] for y in range(ny)]
            values = run(values, fac[1, h], fwd[1, h])
            largest = jnp.full((8, BLOCK), 1e-30, F32)
            for y in range(ny):
                ends[h, y * ZLO : (y + 1) * ZLO, :] = values[y]
                largest = jnp.maximum(largest, jnp.abs(values[y]))
            largest = jnp.max(largest, axis=0, keepdims=True)
            es_send[h] = largest * (1.0 / TOP)
            scale = TOP / largest
            send_ring(h, lambda z: scale, e_send, e_recv, e_sem, True)

        def sweep_y(h):
            def one(x, carry):
                values = [planes[h, x, y * ZLO : (y + 1) * ZLO, :] for y in range(ny)]
                values = run(values, fac[1, h], fwd[1, h])
                for y in range(ny):
                    planes[h, x, y * ZLO : (y + 1) * ZLO, :] = values[y]
                return carry

            lax.fori_loop(0, XLO, one, 0)

        def scan_ring(h):
            leap = fac[0, h] * fac[0, h]
            leap = leap * leap
            f = fwd[0, h]

            def exclusive(given):
                ordered = [jnp.where(f, given[s], given[nz_dev - 1 - s]) for s in range(nz_dev)]
                taken = [jnp.zeros_like(ordered[0])]
                for s in range(nz_dev - 1):
                    taken.append(leap * taken[-1] + ordered[s])
                return [jnp.where(f, taken[z], taken[nz_dev - 1 - z]) for z in range(nz_dev)]

            bounds = exclusive([jnp.broadcast_to(es_recv[h, z], (8, BLOCK)) for z in range(nz_dev)])
            for z in range(nz_dev):
                bound[h, z] = bounds[z][:1]
            for part in range(per_z // 16):
                got = [
                    decode(e_recv[h, z, part * 16 : part * 16 + 16, :]) * es_recv[h, z] for z in range(nz_dev)
                ]
                for i in range(2):
                    taken = exclusive([g[i * 8 : i * 8 + 8] for g in got])
                    for z in range(nz_dev):
                        start = z * per_z + part * 16 + i * 8
                        ends[h, start : start + 8, :] = taken[z]
            send_ring(h, lambda z: 1.0 / jnp.maximum(bound[h, z], 1e-36), b_send, b_recv, b_sem, False)

        def finish_half(h):
            def inflow(z, carry):
                ends[h, pl.ds(z * per_z, per_z), :] = decode(b_recv[h, z]) * bound[h, me_z]
                return carry

            lax.fori_loop(0, nz_dev, inflow, 0)

            def finish(j, carry):
                m = mode_at(j)
                rows = pl.ds(m * YLO * ZLO, YLO * ZLO)
                t, f = wide_fac(h), wide_fwd(h)
                given = [planes[h, x, rows, :] for x in range(XLO)]
                value = ends[h, rows, :]
                swept = []
                for x in range(XLO):
                    value = t * value + jnp.where(f, given[x], given[XLO - 1 - x])
                    swept.append(value)
                for x in range(XLO):
                    result = jnp.where(f, swept[x], swept[XLO - 1 - x]).astype(BF16)
                    if last:
                        f_send[h, x, rows, :] = result
                    else:
                        c_send[h, m * ny_dev + x] = result
                if not last:
                    for i in range(ny_dev):
                        y = y_at(i)
                        to = (me_z * ny_dev + y, m)
                        into = cur_b.at[h, me_m, pl.ds(me_y * YLO * ZLO, YLO * ZLO), :]

                        def send():
                            remote(c_send.at[h, m * ny_dev + y], into, c_sem.at[h], c_sem.at[2 + h], to).start()

                        def keep():
                            pltpu.make_async_copy(c_send.at[h, m * ny_dev + y], into, c_sem.at[2 + h]).start()

                        if i < ny_dev - 1:
                            send()
                        else:
                            pl.when(j < nm - 1)(send)
                            pl.when(j == nm - 1)(keep)
                return carry

            lax.fori_loop(0, nm, finish, 0)
            if last:
                for i in range(ny_dev - 1):
                    y = y_at(i)
                    to = (me_z * ny_dev + y, me_m)
                    remote(f_send.at[h, y], f_recv.at[h, me_y], f_sem.at[h], f_sem.at[2 + h], to).start()
                pltpu.make_async_copy(f_send.at[h, me_y], f_recv.at[h, me_y], f_sem.at[2 + h]).start()

        await_bytes(x_recv.at[0], x_sem.at[2])
        await_bytes(xs_recv, scale_sem.at[1])
        if iteration == 0:
            await_bytes(s_recv, s0_recv.at[1])
            await_bytes(ss_recv, s0_recv.at[3])
        hand_on(0)
        await_bytes(x_recv.at[1], x_sem.at[3])
        hand_on(1)
        sweep_y(0)
        for h in range(2):
            await_bytes(e_recv.at[h], e_sem.at[2 + h])
            await_bytes(es_recv.at[h], scale_sem.at[4 + h])
            scan_ring(h)
            if h == 0:
                sweep_y(1)
        for h in range(2):
            await_bytes(b_recv.at[h], b_sem.at[2 + h])
            finish_half(h)
        await_bytes(xs_recv.at[pl.ds(0, group - 1)], scale_sem.at[0])
        for h in range(2):
            await_bytes(x_send.at[h, pl.ds(0, group - 1)], x_sem.at[h])
            await_bytes(e_send.at[h, pl.ds(0, nz_dev - 1)], e_sem.at[h])
            await_bytes(es_recv.at[h, pl.ds(0, nz_dev - 1)], scale_sem.at[2 + h])
            await_bytes(b_send.at[h, pl.ds(0, nz_dev - 1)], b_sem.at[h])
        if not last:
            for h in range(2):
                await_bytes(cur_b.at[h], c_sem.at[2 + h])
                await_bytes(c_send.at[h, pl.ds(0, group - 1)], c_sem.at[h])

    await_bytes(turned.at[pl.ds(0, nm - 1)], s0_send.at[0])
    await_bytes(s_send.at[pl.ds(0, ny_dev - 1)], s0_send.at[1])
    await_bytes(ss_recv.at[pl.ds(0, ny_dev - 1)], s0_send.at[3])
    await_bytes(coef.at[pl.ds(0, nm - 1)], s0_send.at[2])
    if chips > 1:
        await_bytes(blocks.at[0, pl.ds(0, chips - 1)], gather_send.at[0])
        await_bytes(blocks.at[pl.ds(0, chips - 1), direct], gather_send.at[1])
        await_bytes(blocks.at[pl.ds(0, chips - 1), pl.ds(0, ny_dev - 1)], gather_send.at[3])
        await_bytes(blocks.at[pl.ds(0, chips - 1)], gather_send.at[4])
    await_bytes(blocks.at[0], gather_send.at[2])
    wide = identity(BLOCK)
    for h in range(2):
        await_bytes(f_recv.at[h], f_sem.at[2 + h])
        for m in range(nm):
            parts = [f_recv[h, zh, m * YLO * ZLO : (m + 1) * YLO * ZLO, :].astype(F32) for zh in range(ny_dev)]
            rows = [parts[zh][y * ZLO : (y + 1) * ZLO] for y in range(YLO) for zh in range(ny_dev)]
            tile = jnp.concatenate(rows, axis=0).astype(BF16)
            out[h * BLOCK : (h + 1) * BLOCK, m * chunk : (m + 1) * chunk] = nt(wide, tile).astype(BF16)
    for h in range(2):
        await_bytes(f_send.at[h, pl.ds(0, ny_dev - 1)], f_sem.at[h])


def local(dims, source, prior, coupling, pairs, transmission, direction):
    nm, ny_dev, nz_dev, ny, nz = dims
    modes = source.shape[0]
    group = nm * ny_dev
    chunk = YLO * nz
    tall = ny * ZLO
    per_z = tall // nz_dev
    vmem = pl.BlockSpec(memory_space=pltpu.VMEM)
    hbm = pl.BlockSpec(memory_space=pltpu.HBM)
    dma = pltpu.SemaphoreType.DMA
    result = pl.pallas_call(
        functools.partial(kernel, dims),
        out_shape=jax.ShapeDtypeStruct((modes, ny * nz), BF16),
        in_specs=[hbm] * 6,
        out_specs=vmem,
        scratch_shapes=[
            pltpu.SMEM((PER_ROW, 2 * nm), jnp.int32),
            pltpu.VMEM((3, modes), F32),
            pltpu.VMEM((3, modes), jnp.int32),
            pltpu.VMEM((modes, ny * nz), BF16),
            pltpu.VMEM((modes, ny * nz), BF16),
            pltpu.VMEM((2, nm, chunk, BLOCK), BF16),
            pltpu.VMEM((2, nm, chunk, BLOCK), BF16),
            pltpu.VMEM((nm, 2, chunk, BLOCK), BF16),
            pltpu.VMEM((ny_dev, 2, tall, BLOCK), I16),
            pltpu.VMEM((ny_dev, 2, tall, BLOCK), I16),
            pltpu.VMEM((nm, 1, BLOCK), F32),
            pltpu.VMEM((ny_dev, nm, 1, BLOCK), F32),
            pltpu.VMEM((nm, 2 * PER_ROW, BLOCK, BLOCK), BF16),
            pltpu.VMEM((2, 8, BLOCK), F32),
            pltpu.VMEM((nm, 2, 8, BLOCK), F32),
            pltpu.VMEM((2 * chunk, BLOCK), F32),
            pltpu.VMEM((2, group, YLO * ZLO, BLOCK), I16),
            pltpu.VMEM((2, group, YLO * ZLO, BLOCK), I16),
            pltpu.VMEM((nm, 1, BLOCK), F32),
            pltpu.VMEM((group, 1, BLOCK), F32),
            pltpu.VMEM((2, XLO, tall, BLOCK), F32),
            pltpu.VMEM((2, tall, BLOCK), F32),
            pltpu.VMEM((2, nz_dev, per_z, BLOCK), I16),
            pltpu.VMEM((2, nz_dev, per_z, BLOCK), I16),
            pltpu.VMEM((2, 1, BLOCK), F32),
            pltpu.VMEM((2, nz_dev, 1, BLOCK), F32),
            pltpu.VMEM((2, nz_dev, per_z, BLOCK), I16),
            pltpu.VMEM((2, nz_dev, per_z, BLOCK), I16),
            pltpu.VMEM((2, nz_dev, 1, BLOCK), F32),
            pltpu.VMEM((2, group, YLO * ZLO, BLOCK), BF16),
            pltpu.VMEM((2, ny_dev, tall, BLOCK), BF16),
            pltpu.VMEM((2, ny_dev, tall, BLOCK), BF16),
            pltpu.SemaphoreType.REGULAR((4,)),
            dma((6,)),
            dma((4,)),
            dma((4,)),
            dma((5,)),
            dma((2,)),
            dma((nm // 2,)),
            dma((nm // 2,)),
            dma((4,)),
            dma((4,)),
            dma((4,)),
            dma((4,)),
            dma((4,)),
            dma((6,)),
        ],
        compiler_params=pltpu.CompilerParams(
            collective_id=0, has_side_effects=True, vmem_limit_bytes=60 * 1024 * 1024
        ),
        cost_estimate=pl.CostEstimate(flops=600_000_000, bytes_accessed=2_000_000, transcendentals=0),
    )(
        source.reshape(modes, ny * nz),
        prior.reshape(modes, ny * nz),
        coupling.reshape(2 * PER_ROW, BLOCK, BLOCK),
        pairs.T,
        transmission,
        direction,
    )
    return result.reshape(modes, 1, ny * nz)


def build(mesh, ny, nz):
    nm = mesh.shape["mode"]
    ny_dev = nz // ZLO
    nz_dev = mesh.shape["cell"] // ny_dev
    in_specs = (
        P("mode", "cell", None),
        P("mode", "cell", None),
        P("mode", None, None, None),
        P(),
        P(None, "mode"),
        P(None, "mode"),
    )
    body = functools.partial(local, (nm, ny_dev, nz_dev, ny, nz))
    return jax.shard_map(body, mesh=mesh, in_specs=in_specs, out_specs=P("mode", "cell", None), check_vma=False)


def solution(mesh):
    return build(mesh, 32, 32)
```

```python
import functools

import jax
import jax.numpy as jnp
from jax import lax
from jax.experimental import pallas as pl
from jax.experimental.pallas import tpu as pltpu
from jax.sharding import PartitionSpec as P

ITERS = 2
BLOCK = 128
PER_ROW = 4
ZLO = 8
YLO = 4
XLO = 4
TOP = 32767.0
F32 = jnp.float32
BF16 = jnp.bfloat16
I16 = jnp.int16
MESH = pl.DeviceIdType.MESH


def nt(left, right):
    return lax.dot_general(left, right, (((1,), (1,)), ((), ())), preferred_element_type=F32)


def identity(size):
    rows = lax.broadcasted_iota(jnp.int32, (size, size), 0)
    columns = lax.broadcasted_iota(jnp.int32, (size, size), 1)
    return jnp.where(rows == columns, 1.0, 0.0).astype(BF16)


def run(values, factor, forward):
    n = len(values)
    ordered = [jnp.where(forward, values[s], values[n - 1 - s]) for s in range(n)]
    swept = [ordered[0]]
    for s in range(1, n):
        swept.append(factor * swept[-1] + ordered[s])
    return [jnp.where(forward, swept[s], swept[n - 1 - s]) for s in range(n)]


def farthest_first(j, n):
    if isinstance(j, int):
        return (n // 2 + (j // 2 if j % 2 == 0 else -((j + 1) // 2))) % n
    return n // 2 + jnp.where(j % 2 == 0, j // 2, -((j + 1) // 2)) + n


def encode(values, scale):
    return jnp.round(values * scale).astype(jnp.int32).astype(I16)


def decode(codes):
    return codes.astype(jnp.int32).astype(F32)


def kernel(
    dims,
    source,
    prior,
    coupling,
    pairs_in,
    transmission_in,
    direction_in,
    out,
    pairs,
    transmission,
    direction,
    source_v,
    prior_v,
    cur_a,
    cur_b,
    turned,
    s_send,
    s_recv,
    ss_send,
    ss_recv,
    blocks,
    coef_own,
    coef,
    work,
    xscale,
    x_send,
    x_recv,
    xs_send,
    xs_recv,
    planes,
    ends,
    e_send,
    e_recv,
    es_send,
    es_recv,
    b_send,
    b_recv,
    bound,
    c_send,
    f_send,
    f_recv,
    round_sem,
    in_sem,
    s0_send,
    s0_recv,
    gather_send,
    gather_recv,
    direct_sem,
    part_sem,
    x_sem,
    e_sem,
    b_sem,
    c_sem,
    f_sem,
    scale_sem,
):
    nm, ny_dev, nz_dev, ny, nz = dims
    chips = nm // 2
    chunk = YLO * nz
    tall = ny * ZLO
    per_z = tall // nz_dev
    me_m = lax.axis_index("mode")
    me_c = lax.axis_index("cell")
    me_z, me_y = me_c // ny_dev, me_c % ny_dev
    me_x, me_core = me_m // 2, me_m % 2

    def remote(src, dst, send, recv, to):
        return pltpu.make_async_remote_copy(
            src_ref=src, dst_ref=dst, send_sem=send, recv_sem=recv, device_id=to, device_id_type=MESH
        )

    def mode_at(j):
        x = (me_x + farthest_first(j // 2, chips)) % chips
        return x * 2 + (me_core + 1 + j % 2) % 2

    def y_at(i):
        return (me_y + farthest_first(i, ny_dev)) % ny_dev

    def await_bytes(ref, sem):
        pltpu.make_async_copy(ref, ref, sem).wait()

    loads = [
        pltpu.make_async_copy(prior, prior_v, in_sem.at[0]),
        pltpu.make_async_copy(coupling, blocks.at[me_m], in_sem.at[1]),
        pltpu.make_async_copy(source, source_v, in_sem.at[2]),
    ]
    small = [
        pltpu.make_async_copy(transmission_in, transmission, in_sem.at[3]),
        pltpu.make_async_copy(direction_in, direction, in_sem.at[4]),
        pltpu.make_async_copy(pairs_in, pairs, in_sem.at[5]),
    ]

    barrier = pltpu.get_barrier_semaphore()
    group = nm * ny_dev
    near = [(me_z * ny_dev + (me_y + i) % ny_dev, me_m) for i in range(1, ny_dev)]
    near += [(me_c, (me_m + j) % nm) for j in range(1, nm)]

    def ring(step):
        return [((me_z + z) % nz_dev * ny_dev + me_y, me_m) for z in sorted({step % nz_dev, -step % nz_dev} - {0})]

    near += ring(1)
    for to in near:
        pl.semaphore_signal(barrier, inc=1, device_id=to, device_id_type=MESH)
    for load in small + loads:
        load.start()

    rounds = []
    while 2 ** len(rounds) < nz_dev // 2:
        rounds.append(2 ** len(rounds))

    def meet(r):
        if r and r - 1 < len(rounds):
            pl.semaphore_wait(round_sem.at[r - 1], 2)
        if r < len(rounds):
            for to in ring(rounds[r]):
                pl.semaphore_signal(round_sem.at[r], inc=1, device_id=to, device_id_type=MESH)

    for load in small:
        load.wait()
    fwd = {}
    fac = {}
    weight = {}
    for h in range(2):
        lanes = slice(h * BLOCK, (h + 1) * BLOCK)
        for d in range(3):
            fac[d, h] = jnp.broadcast_to(transmission[d : d + 1, lanes], (8, BLOCK))
            fwd[d, h] = jnp.broadcast_to(direction[d : d + 1, lanes], (8, BLOCK)) == 1
        total = jnp.sqrt(1.0 - transmission[0:1, lanes] * transmission[0:1, lanes])
        for d in range(1, 3):
            total = total * jnp.sqrt(1.0 - transmission[d : d + 1, lanes] * transmission[d : d + 1, lanes])
        weight[h] = total
    for h in range(2):
        coef_own[0, h * 4 : h * 4 + 4, :] = fac[2, h][:4]
        coef_own[1, h * 4 : h * 4 + 4, :] = jnp.where(fwd[2, h], 1.0, 0.0)[:4]

    eye = identity(chunk)

    loads[0].wait()
    for m in range(nm):
        for h in range(2):
            tile = nt(eye, prior_v[h * BLOCK : (h + 1) * BLOCK, m * chunk : (m + 1) * chunk])
            rows = [
                tile[y * nz + zh * ZLO : y * nz + (zh + 1) * ZLO] for zh in range(ny_dev) for y in range(YLO)
            ]
            turned[m, h] = jnp.concatenate(rows, axis=0).astype(BF16)

    def sweep_z(m, factor, forward):
        values = run([work[m, pl.ds(z, 8, stride=nz), :] for z in range(nz)], factor, forward)
        largest = jnp.abs(values[0])
        for z in range(nz):
            work[m, pl.ds(z, 8, stride=nz), :] = values[z]
            if z:
                largest = jnp.maximum(largest, jnp.abs(values[z]))
        largest = jnp.maximum(jnp.max(largest, axis=0, keepdims=True), 1e-30)
        return TOP / largest, largest * (1.0 / TOP)

    def two_rows(m, h, y, zh):
        start = h * chunk + y * nz + zh * ZLO
        return jnp.concatenate([work[m, start : start + ZLO, :], work[m, start + nz : start + nz + ZLO, :]], axis=0)

    loads[1].wait()
    pl.semaphore_wait(barrier, len(near))
    meet(0)

    sibling = me_x * 2 + 1 - me_core
    shared = pl.ds(PER_ROW + me_y, 1)
    direct = pl.ds(0, PER_ROW)
    for j in [farthest_first(i, chips) for i in range(chips - 1)]:
        to = (me_c, ((me_x + j) % chips) * 2 + me_core)
        part = blocks.at[me_m, shared]
        remote(part, part, gather_send.at[0], part_sem.at[j], to).start()
    for j in [farthest_first(i, chips) for i in range(chips - 1)]:
        to = (me_c, ((me_x + j) % chips) * 2 + me_core)
        part = blocks.at[me_m, direct]
        remote(part, part, gather_send.at[1], direct_sem.at[j], to).start()
    pltpu.make_async_copy(turned.at[me_m], cur_a.at[:, me_m], s0_recv.at[0]).start()
    for j in range(nm - 1):
        m = mode_at(j)
        remote(turned.at[m], cur_a.at[:, me_m], s0_send.at[0], s0_recv.at[0], (me_c, m)).start()
    pltpu.make_async_copy(coef_own, coef.at[me_m], s0_recv.at[2]).start()
    for j in range(nm - 1):
        m = mode_at(j)
        remote(coef_own, coef.at[me_m], s0_send.at[2], s0_recv.at[2], (me_c, m)).start()
    own = blocks.at[me_m]
    remote(own, own, gather_send.at[2], gather_recv.at[1], (me_c, sibling)).start()

    def over_y(m):
        part = blocks.at[m, shared]
        for i in range(ny_dev - 1):
            to = (me_z * ny_dev + y_at(i), me_m)
            remote(part, part, gather_send.at[3], gather_recv.at[0], to).start()

    meet(1)
    for j in [farthest_first(i, chips) for i in range(chips - 1)]:
        m = ((me_x + chips - j) % chips) * 2 + me_core
        await_bytes(blocks.at[m, shared], part_sem.at[j])
        over_y(m)

    meet(2)
    loads[2].wait()

    def sweep_source(m, carry):
        for h in range(2):
            columns = pl.ds(pl.multiple_of(m * chunk, chunk), chunk)
            work[m, h * chunk : (h + 1) * chunk, :] = nt(eye, source_v[h * BLOCK : (h + 1) * BLOCK, columns])
        scale, unit = sweep_z(m, coef_own[0], coef_own[1] > 0.5)
        ss_send[m] = unit
        for zh in range(ny_dev):
            for h in range(2):
                for y in range(0, YLO, 2):
                    rows = pl.ds(m * YLO * ZLO + y * ZLO, 2 * ZLO)
                    s_send[zh, h, rows, :] = encode(two_rows(m, h, y, zh), scale)
        return carry

    lax.fori_loop(0, nm, sweep_source, 0)
    for i in range(ny_dev - 1):
        y = y_at(i)
        to = (me_z * ny_dev + y, me_m)
        remote(s_send.at[y], s_recv.at[me_y], s0_send.at[1], s0_recv.at[1], to).start()
        remote(ss_send, ss_recv.at[me_y], s0_send.at[3], s0_recv.at[3], to).start()
    pltpu.make_async_copy(s_send.at[me_y], s_recv.at[me_y], s0_recv.at[1]).start()
    pltpu.make_async_copy(ss_send, ss_recv.at[me_y], s0_recv.at[3]).start()
    for j in range(1, chips):
        part = blocks.at[((me_x + chips - j) % chips) * 2 + me_core, direct]
        await_bytes(part, direct_sem.at[j])
        remote(part, part, gather_send.at[4], gather_recv.at[1], (me_c, sibling)).start()
    if chips > 1:
        await_bytes(blocks.at[pl.ds(0, chips - 1), pl.ds(0, ny_dev - 1)], gather_recv.at[0])
    for j in range(1, chips):
        part = blocks.at[((me_x + chips - j) % chips) * 2 + me_core, pl.ds(PER_ROW, PER_ROW)]
        remote(part, part, gather_send.at[4], gather_recv.at[1], (me_c, sibling)).start()
    meet(3)
    await_bytes(cur_a, s0_recv.at[0])
    await_bytes(coef, s0_recv.at[2])
    await_bytes(blocks.at[pl.ds(0, chips)], gather_recv.at[1])

    for iteration in range(ITERS):
        current = cur_a if iteration == 0 else cur_b
        last = iteration == ITERS - 1

        def scatter(j, carry):
            m = mode_at(j)
            for h in range(2):
                row = m * 2 + h
                left = jnp.concatenate([current[pairs[k, row] % 2, pairs[k, row] // 2] for k in range(PER_ROW)], axis=1)
                right = jnp.concatenate([blocks[m, h * PER_ROW + k] for k in range(PER_ROW)], axis=1)
                total = nt(left, right)
                for zh in range(ny_dev):
                    for y in range(YLO):
                        work[m, h * chunk + y * nz + zh * ZLO : h * chunk + y * nz + (zh + 1) * ZLO, :] = total[
                            (zh * YLO + y) * ZLO : (zh * YLO + y + 1) * ZLO
                        ]
            scale, unit = sweep_z(m, coef[m, 0], coef[m, 1] > 0.5)
            xs_send[m] = unit
            xscale[m] = scale
            code(m, 0)
            send_codes(j, 0, True)
            return carry

        def send_codes(j, h, with_scale):
            m = mode_at(j)
            slot = me_m * ny_dev + me_y
            for i in range(ny_dev):
                y = y_at(i)
                to = (me_z * ny_dev + y, m)

                def send():
                    src, dst = x_send.at[h, m * ny_dev + y], x_recv.at[h, slot]
                    remote(src, dst, x_sem.at[h], x_sem.at[2 + h], to).start()
                    if with_scale:
                        remote(xs_send.at[m], xs_recv.at[slot], scale_sem.at[0], scale_sem.at[1], to).start()

                def keep():
                    src, dst = x_send.at[h, m * ny_dev + y], x_recv.at[h, slot]
                    pltpu.make_async_copy(src, dst, x_sem.at[2 + h]).start()
                    if with_scale:
                        pltpu.make_async_copy(xs_send.at[m], xs_recv.at[slot], scale_sem.at[1]).start()

                if i < ny_dev - 1:
                    send()
                else:
                    pl.when(j < nm - 1)(send)
                    pl.when(j == nm - 1)(keep)

        def code(m, h):
            for zh in range(ny_dev):
                for y in range(0, YLO, 2):
                    rows = two_rows(m, h, y, zh)
                    x_send[h, m * ny_dev + zh, y * ZLO : (y + 2) * ZLO, :] = encode(rows, xscale[m])

        def send_second(j, carry):
            code(mode_at(j), 1)
            send_codes(j, 1, False)
            return carry

        lax.fori_loop(0, nm, scatter, 0)
        lax.fori_loop(0, nm, send_second, 0)

        def send_ring(h, scale_of, codes, into, sem, with_unit):
            def one(j, carry):
                z = (me_z + farthest_first(j, nz_dev)) % nz_dev
                codes[h, z] = encode(ends[h, pl.ds(z * per_z, per_z), :], scale_of(z))
                to = (z * ny_dev + me_y, me_m)

                @pl.when(j < nz_dev - 1)
                def _():
                    remote(codes.at[h, z], into.at[h, me_z], sem.at[h], sem.at[2 + h], to).start()
                    if with_unit:
                        remote(
                            es_send.at[h], es_recv.at[h, me_z], scale_sem.at[2 + h], scale_sem.at[4 + h], to
                        ).start()

                @pl.when(j == nz_dev - 1)
                def _():
                    pltpu.make_async_copy(codes.at[h, z], into.at[h, me_z], sem.at[2 + h]).start()
                    if with_unit:
                        pltpu.make_async_copy(es_send.at[h], es_recv.at[h, me_z], scale_sem.at[4 + h]).start()

                return carry

            lax.fori_loop(0, nz_dev, one, 0)

        def wide_fac(h):
            return jnp.concatenate([fac[0, h]] * YLO, axis=0)

        def wide_fwd(h):
            tile = jnp.broadcast_to(direction[0:1, h * BLOCK : (h + 1) * BLOCK], (8, BLOCK))
            return jnp.concatenate([tile] * YLO, axis=0) == 1

        def hand_on(h):
            def unpack(m, carry):
                rows = pl.ds(m * YLO * ZLO, YLO * ZLO)
                got = []
                for x in range(XLO):
                    value = decode(x_recv[h, m * ny_dev + x]) * (xs_recv[m * ny_dev + x] * weight[h])
                    value += decode(s_recv[x, h, rows, :]) * (ss_recv[x, m] * weight[h])
                    planes[h, x, rows, :] = value
                    got.append(value)
                t, f = wide_fac(h), wide_fwd(h)
                end = jnp.where(f, got[0], got[XLO - 1])
                for x in range(1, XLO):
                    end = end * t + jnp.where(f, got[x], got[XLO - 1 - x])
                ends[h, rows, :] = end
                return carry

            lax.fori_loop(0, nm, unpack, 0)
            values = [ends[h, y * ZLO : (y + 1) * ZLO, :] for y in range(ny)]
            values = run(values, fac[1, h], fwd[1, h])
            largest = jnp.full((8, BLOCK), 1e-30, F32)
            for y in range(ny):
                ends[h, y * ZLO : (y + 1) * ZLO, :] = values[y]
                largest = jnp.maximum(largest, jnp.abs(values[y]))
            largest = jnp.max(largest, axis=0, keepdims=True)
            es_send[h] = largest * (1.0 / TOP)
            scale = TOP / largest
            send_ring(h, lambda z: scale, e_send, e_recv, e_sem, True)

        def sweep_y(h):
            def one(x, carry):
                values = [planes[h, x, y * ZLO : (y + 1) * ZLO, :] for y in range(ny)]
                values = run(values, fac[1, h], fwd[1, h])
                for y in range(ny):
                    planes[h, x, y * ZLO : (y + 1) * ZLO, :] = values[y]
                return carry

            lax.fori_loop(0, XLO, one, 0)

        def scan_ring(h):
            leap = fac[0, h] * fac[0, h]
            leap = leap * leap
            f = fwd[0, h]

            def exclusive(given):
                ordered = [jnp.where(f, given[s], given[nz_dev - 1 - s]) for s in range(nz_dev)]
                taken = [jnp.zeros_like(ordered[0])]
                for s in range(nz_dev - 1):
                    taken.append(leap * taken[-1] + ordered[s])
                return [jnp.where(f, taken[z], taken[nz_dev - 1 - z]) for z in range(nz_dev)]

            bounds = exclusive([jnp.broadcast_to(es_recv[h, z], (8, BLOCK)) for z in range(nz_dev)])
            for z in range(nz_dev):
                bound[h, z] = bounds[z][:1]
            for part in range(per_z // 16):
                got = [
                    decode(e_recv[h, z, part * 16 : part * 16 + 16, :]) * es_recv[h, z] for z in range(nz_dev)
                ]
                for i in range(2):
                    taken = exclusive([g[i * 8 : i * 8 + 8] for g in got])
                    for z in range(nz_dev):
                        start = z * per_z + part * 16 + i * 8
                        ends[h, start : start + 8, :] = taken[z]
            send_ring(h, lambda z: 1.0 / jnp.maximum(bound[h, z], 1e-36), b_send, b_recv, b_sem, False)

        def finish_half(h):
            def inflow(z, carry):
                ends[h, pl.ds(z * per_z, per_z), :] = decode(b_recv[h, z]) * bound[h, me_z]
                return carry

            lax.fori_loop(0, nz_dev, inflow, 0)

            def finish(j, carry):
                m = mode_at(j)
                rows = pl.ds(m * YLO * ZLO, YLO * ZLO)
                t, f = wide_fac(h), wide_fwd(h)
                given = [planes[h, x, rows, :] for x in range(XLO)]
                value = ends[h, rows, :]
                swept = []
                for x in range(XLO):
                    value = t * value + jnp.where(f, given[x], given[XLO - 1 - x])
                    swept.append(value)
                for x in range(XLO):
                    result = jnp.where(f, swept[x], swept[XLO - 1 - x]).astype(BF16)
                    if last:
                        f_send[h, x, rows, :] = result
                    else:
                        c_send[h, m * ny_dev + x] = result
                if not last:
                    for i in range(ny_dev):
                        y = y_at(i)
                        to = (me_z * ny_dev + y, m)
                        into = cur_b.at[h, me_m, pl.ds(me_y * YLO * ZLO, YLO * ZLO), :]

                        def send():
                            remote(c_send.at[h, m * ny_dev + y], into, c_sem.at[h], c_sem.at[2 + h], to).start()

                        def keep():
                            pltpu.make_async_copy(c_send.at[h, m * ny_dev + y], into, c_sem.at[2 + h]).start()

                        if i < ny_dev - 1:
                            send()
                        else:
                            pl.when(j < nm - 1)(send)
                            pl.when(j == nm - 1)(keep)
                return carry

            lax.fori_loop(0, nm, finish, 0)
            if last:
                for i in range(ny_dev - 1):
                    y = y_at(i)
                    to = (me_z * ny_dev + y, me_m)
                    remote(f_send.at[h, y], f_recv.at[h, me_y], f_sem.at[h], f_sem.at[2 + h], to).start()
                pltpu.make_async_copy(f_send.at[h, me_y], f_recv.at[h, me_y], f_sem.at[2 + h]).start()

        await_bytes(x_recv.at[0], x_sem.at[2])
        await_bytes(xs_recv, scale_sem.at[1])
        if iteration == 0:
            await_bytes(s_recv, s0_recv.at[1])
            await_bytes(ss_recv, s0_recv.at[3])
        hand_on(0)
        await_bytes(x_recv.at[1], x_sem.at[3])
        hand_on(1)
        sweep_y(0)
        for h in range(2):
            await_bytes(e_recv.at[h], e_sem.at[2 + h])
            await_bytes(es_recv.at[h], scale_sem.at[4 + h])
            scan_ring(h)
            if h == 0:
                sweep_y(1)
        for h in range(2):
            await_bytes(b_recv.at[h], b_sem.at[2 + h])
            finish_half(h)
        await_bytes(xs_recv.at[pl.ds(0, group - 1)], scale_sem.at[0])
        for h in range(2):
            await_bytes(x_send.at[h, pl.ds(0, group - 1)], x_sem.at[h])
            await_bytes(e_send.at[h, pl.ds(0, nz_dev - 1)], e_sem.at[h])
            await_bytes(es_recv.at[h, pl.ds(0, nz_dev - 1)], scale_sem.at[2 + h])
            await_bytes(b_send.at[h, pl.ds(0, nz_dev - 1)], b_sem.at[h])
        if not last:
            for h in range(2):
                await_bytes(cur_b.at[h], c_sem.at[2 + h])
                await_bytes(c_send.at[h, pl.ds(0, group - 1)], c_sem.at[h])

    await_bytes(turned.at[pl.ds(0, nm - 1)], s0_send.at[0])
    await_bytes(s_send.at[pl.ds(0, ny_dev - 1)], s0_send.at[1])
    await_bytes(ss_recv.at[pl.ds(0, ny_dev - 1)], s0_send.at[3])
    await_bytes(coef.at[pl.ds(0, nm - 1)], s0_send.at[2])
    if chips > 1:
        await_bytes(blocks.at[0, pl.ds(0, chips - 1)], gather_send.at[0])
        await_bytes(blocks.at[pl.ds(0, chips - 1), direct], gather_send.at[1])
        await_bytes(blocks.at[pl.ds(0, chips - 1), pl.ds(0, ny_dev - 1)], gather_send.at[3])
        await_bytes(blocks.at[pl.ds(0, chips - 1)], gather_send.at[4])
    await_bytes(blocks.at[0], gather_send.at[2])
    wide = identity(BLOCK)
    for h in range(2):
        await_bytes(f_recv.at[h], f_sem.at[2 + h])
        for m in range(nm):
            parts = [f_recv[h, zh, m * YLO * ZLO : (m + 1) * YLO * ZLO, :].astype(F32) for zh in range(ny_dev)]
            rows = [parts[zh][y * ZLO : (y + 1) * ZLO] for y in range(YLO) for zh in range(ny_dev)]
            tile = jnp.concatenate(rows, axis=0).astype(BF16)
            out[h * BLOCK : (h + 1) * BLOCK, m * chunk : (m + 1) * chunk] = nt(wide, tile).astype(BF16)
    for h in range(2):
        await_bytes(f_send.at[h, pl.ds(0, ny_dev - 1)], f_sem.at[h])


def local(dims, source, prior, coupling, pairs, transmission, direction):
    nm, ny_dev, nz_dev, ny, nz = dims
    modes = source.shape[0]
    group = nm * ny_dev
    chunk = YLO * nz
    tall = ny * ZLO
    per_z = tall // nz_dev
    vmem = pl.BlockSpec(memory_space=pltpu.VMEM)
    hbm = pl.BlockSpec(memory_space=pltpu.HBM)
    dma = pltpu.SemaphoreType.DMA
    result = pl.pallas_call(
        functools.partial(kernel, dims),
        out_shape=jax.ShapeDtypeStruct((modes, ny * nz), BF16),
        in_specs=[hbm] * 6,
        out_specs=vmem,
        scratch_shapes=[
            pltpu.SMEM((PER_ROW, 2 * nm), jnp.int32),
            pltpu.VMEM((3, modes), F32),
            pltpu.VMEM((3, modes), jnp.int32),
            pltpu.VMEM((modes, ny * nz), BF16),
            pltpu.VMEM((modes, ny * nz), BF16),
            pltpu.VMEM((2, nm, chunk, BLOCK), BF16),
            pltpu.VMEM((2, nm, chunk, BLOCK), BF16),
            pltpu.VMEM((nm, 2, chunk, BLOCK), BF16),
            pltpu.VMEM((ny_dev, 2, tall, BLOCK), I16),
            pltpu.VMEM((ny_dev, 2, tall, BLOCK), I16),
            pltpu.VMEM((nm, 1, BLOCK), F32),
            pltpu.VMEM((ny_dev, nm, 1, BLOCK), F32),
            pltpu.VMEM((nm, 2 * PER_ROW, BLOCK, BLOCK), BF16),
            pltpu.VMEM((2, 8, BLOCK), F32),
            pltpu.VMEM((nm, 2, 8, BLOCK), F32),
            pltpu.VMEM((nm, 2 * chunk, BLOCK), F32),
            pltpu.VMEM((nm, 1, BLOCK), F32),
            pltpu.VMEM((2, group, YLO * ZLO, BLOCK), I16),
            pltpu.VMEM((2, group, YLO * ZLO, BLOCK), I16),
            pltpu.VMEM((nm, 1, BLOCK), F32),
            pltpu.VMEM((group, 1, BLOCK), F32),
            pltpu.VMEM((2, XLO, tall, BLOCK), F32),
            pltpu.VMEM((2, tall, BLOCK), F32),
            pltpu.VMEM((2, nz_dev, per_z, BLOCK), I16),
            pltpu.VMEM((2, nz_dev, per_z, BLOCK), I16),
            pltpu.VMEM((2, 1, BLOCK), F32),
            pltpu.VMEM((2, nz_dev, 1, BLOCK), F32),
            pltpu.VMEM((2, nz_dev, per_z, BLOCK), I16),
            pltpu.VMEM((2, nz_dev, per_z, BLOCK), I16),
            pltpu.VMEM((2, nz_dev, 1, BLOCK), F32),
            pltpu.VMEM((2, group, YLO * ZLO, BLOCK), BF16),
            pltpu.VMEM((2, ny_dev, tall, BLOCK), BF16),
            pltpu.VMEM((2, ny_dev, tall, BLOCK), BF16),
            pltpu.SemaphoreType.REGULAR((4,)),
            dma((6,)),
            dma((4,)),
            dma((4,)),
            dma((5,)),
            dma((2,)),
            dma((nm // 2,)),
            dma((nm // 2,)),
            dma((4,)),
            dma((4,)),
            dma((4,)),
            dma((4,)),
            dma((4,)),
            dma((6,)),
        ],
        compiler_params=pltpu.CompilerParams(
            collective_id=0, has_side_effects=True, vmem_limit_bytes=60 * 1024 * 1024
        ),
        cost_estimate=pl.CostEstimate(flops=600_000_000, bytes_accessed=2_000_000, transcendentals=0),
    )(
        source.reshape(modes, ny * nz),
        prior.reshape(modes, ny * nz),
        coupling.reshape(2 * PER_ROW, BLOCK, BLOCK),
        pairs.T,
        transmission,
        direction,
    )
    return result.reshape(modes, 1, ny * nz)


def build(mesh, ny, nz):
    nm = mesh.shape["mode"]
    ny_dev = nz // ZLO
    nz_dev = mesh.shape["cell"] // ny_dev
    in_specs = (
        P("mode", "cell", None),
        P("mode", "cell", None),
        P("mode", None, None, None),
        P(),
        P(None, "mode"),
        P(None, "mode"),
    )
    body = functools.partial(local, (nm, ny_dev, nz_dev, ny, nz))
    return jax.shard_map(body, mesh=mesh, in_specs=in_specs, out_specs=P("mode", "cell", None), check_vma=False)


def solution(mesh):
    return build(mesh, 32, 32)
```
